32 devices in a mesh: tm: 8 (over z, x), tile: 4 (over y, core).
Axes of the slice: x: 2, y: 2, z: 4, core: 2. Of those that a mesh axis runs over, the one named last changes fastest.
Arguments:
- frames: bfloat16 [32, 64, 64, 128], P('tm', 'tile'), may hold values from -6 to 6
- cotangent: bfloat16 [32, 64, 64, 128], P('tm', 'tile'), may hold values from -6 to 6
- w_in: bfloat16 [3, 3, 128, 128], replicated, may hold values from -0.1875 to 0.1875
- w_out: bfloat16 [3, 3, 128, 128], replicated, may hold values from -0.1875 to 0.1875
- skip: float32 [128], replicated, may hold values from 0.5 to 1.5
- log_decay: float32 [32, 128], P('tm'), may hold values from -1 to 0
Outputs:
- output: bfloat16 [32, 64, 64, 128], P('tm', 'tile')
- grad_frames: bfloat16 [32, 64, 64, 128], P('tm', 'tile')
- grad_w_in: float32 [3, 3, 128, 128], replicated
- grad_w_out: float32 [3, 3, 128, 128], replicated
The draws below stay inside these ranges and needn't reach their ends.
All inputs are finite; a program needn't handle non-finite values.
Results may differ from the reference program's by a relative error of at most 0.0029.
Values may be sent and summed in bfloat16 or wider, within the bound.
No kernel may reach another device: no remote copies, remote signals or barrier semaphores. Data moves between devices by JAX's collectives and lax.ppermute only.
A program may use at most 64 MiB of HBM per device.

```python
import math
import jax
import jax.numpy as jnp
from jax import lax

CH = 128
ST = 128
H = 64
W = 64
FRAMES = 32


def draw_log_decay(key, part):
    keys = jax.random.split(jax.random.fold_in(key, 17), 4)
    lowest = 0.1 / FRAMES
    highest = 1.0 / 25.0
    rates = jnp.exp(jax.random.uniform(keys[0], (ST,), jnp.float32, jnp.log(lowest), jnp.log(highest)))
    rough = jnp.exp(jax.random.uniform(keys[1], (FRAMES, ST), jnp.float32, jnp.log(0.5), jnp.log(2.0)))
    places = jax.random.randint(keys[2], (4,), 0, FRAMES)
    struck = jnp.any(jnp.arange(FRAMES)[:, None] == places[None, :], axis=1)
    losses = jax.random.uniform(keys[3], (FRAMES, ST), jnp.float32, jnp.log(0.5), jnp.log(0.8))
    values = -rates[None, :] * rough + jnp.where(struck[:, None], losses, 0.0)
    return values.astype(jnp.float32)


def block_scale(rng, shape, shards, low, top_value):
    level, own = 1.0, jax.random.fold_in(rng, 6)
    for position, blocks in shards:
        heights = jnp.exp(jax.random.uniform(jax.random.fold_in(own, position), (blocks,), jnp.float32, low / len(shards), top_value / len(shards)))
        level = level * jnp.repeat(heights, shape[position] // blocks).reshape([-1 if axis == position else 1 for axis in range(len(shape))])
    return level


def gaussian(stream_key, shape, spread, limit, shards=(), dtype=jnp.bfloat16):
    factor_of = block_scale(stream_key, shape, shards, -0.22, 0.18) if shards else 1.0
    array = jax.random.normal(stream_key, shape, jnp.float32) * spread * factor_of
    return jnp.minimum(jnp.maximum(array, -limit), limit).astype(dtype)


def setup_inputs(seed: int = 0) -> dict:
    arg_keys = jax.random.split(jax.random.key(seed), 7)
    frames = gaussian(arg_keys[0], (FRAMES, H, W, CH), 1.0, 6.0, ((0, 8), (1, 4)))
    cotangent = gaussian(arg_keys[1], (FRAMES, H, W, CH), 1.0, 6.0, ((0, 8), (1, 4)))
    w_in = gaussian(arg_keys[2], (3, 3, CH, ST), (9 * CH) ** -0.5, 0.1875)
    w_out = gaussian(arg_keys[3], (3, 3, ST, CH), (9 * ST) ** -0.5, 0.1875)
    skip = jnp.clip(jax.random.uniform(arg_keys[4], (CH,), jnp.float32, 0.5, 1.5), 0.5, 1.5)
    log_decay = draw_log_decay(jax.random.fold_in(arg_keys[6], 71), 0)
    return {"frames": frames, "cotangent": cotangent, "w_in": w_in, "w_out": w_out, "skip": skip, "log_decay": log_decay}


def flipped(weight):
    return jnp.transpose(weight[::-1, ::-1], (0, 1, 3, 2))

def widen(field):
    return jnp.pad(field, ((0, 0), (1, 1), (1, 1), (0, 0)))

def convolve(padded, weight):
    rows = padded.shape[1] - 2
    cols = padded.shape[2] - 2
    result = jnp.zeros((padded.shape[0], rows, cols, weight.shape[3]), jnp.float32)
    for row_off in range(3):
        for col_off in range(3):
            piece = padded[:, row_off:row_off + rows, col_off:col_off + cols, :].reshape(-1, weight.shape[2])
            result = result + jnp.dot(piece, weight[row_off, col_off], preferred_element_type=jnp.float32).reshape(result.shape)
    return result

def weight_grad(padded, target):
    rows = target.shape[1]
    cols = target.shape[2]
    flat = target.reshape(-1, target.shape[3])
    pieces = []
    for row_off in range(3):
        line = []
        for col_off in range(3):
            piece = padded[:, row_off:row_off + rows, col_off:col_off + cols, :].reshape(-1, padded.shape[3])
            line.append(lax.dot_general(piece, flat, (((0,), (0,)), ((), ())), preferred_element_type=jnp.float32))
        pieces.append(jnp.stack(line))
    return jnp.stack(pieces)

def reference(frames, cotangent, w_in, w_out, skip, log_decay):
    decay = jnp.exp(log_decay)
    frames_padded = widen(frames)
    drive = convolve(frames_padded, w_in)

    def advance(state, item):
        rate, inflow = item
        state = rate * state + (1.0 - rate) * inflow
        return (state, state)
    start = jnp.zeros(drive.shape[1:], jnp.float32)
    _, states = lax.scan(advance, start, (decay, drive))
    states_padded = widen(states.astype(jnp.bfloat16))
    output = (convolve(states_padded, w_out) + skip * frames.astype(jnp.float32)).astype(jnp.bfloat16)
    state_grad = convolve(widen(cotangent), flipped(w_out))

    def retreat(carry, item):
        rate, grad_here = item
        adjoint = grad_here + carry
        return (rate * adjoint, adjoint)
    _, adjoints = lax.scan(retreat, jnp.zeros(state_grad.shape[1:], jnp.float32), (decay, state_grad), reverse=True)
    inflow_grad = ((1.0 - decay)[:, None, None, :] * adjoints).astype(jnp.bfloat16)
    grad_frames = (convolve(widen(inflow_grad), flipped(w_in)) + skip * cotangent.astype(jnp.float32)).astype(jnp.bfloat16)
    factor = 1.0 / math.sqrt(FRAMES * H * W)
    grad_w_out = weight_grad(states_padded, cotangent) * factor
    grad_w_in = weight_grad(frames_padded, inflow_grad) * factor
    return (output, grad_frames, grad_w_in, grad_w_out)
```

```python
import functools
import math

import jax
import jax.numpy as jnp
from jax import lax
from jax.experimental import pallas as pl
from jax.experimental.pallas import tpu as pltpu
from jax.sharding import PartitionSpec as P

F32 = jnp.float32
BF16 = jnp.bfloat16
VMEM_LIMIT = 40 * 1024 * 1024


def fill_pairs(pairs, field, top, bottom):
    half = field.shape[1] // 2
    ch = field.shape[3]
    pairs[:, 0, :, :ch] = top[:, 0]
    pairs[:, half, :, ch:] = bottom[:, 0]
    for i in range(half):
        pairs[:, i, :, ch:] = field[:, 2 * i]
        pairs[:, i + 1, :, :ch] = field[:, 2 * i + 1]


def fill_pairs_from_pairs(pairs, field, top, bottom):
    half = field.shape[1]
    ch = field.shape[3] // 2
    pairs[:, 0, :, :ch] = top[:, 0]
    pairs[:, half, :, ch:] = bottom[:, 0]
    pairs[:, :half, :, ch:] = field[:, :, :, :ch]
    pairs[:, 1:, :, :ch] = field[:, :, :, ch:]


def column_taps(flat, cols):
    wide = flat.astype(F32)
    count = wide.shape[0]
    col = lax.broadcasted_iota(jnp.int32, wide.shape, 0) % cols
    left = jnp.where(col == 0, 0.0, pltpu.roll(wide, 1, 0)).astype(flat.dtype)
    right = jnp.where(col == cols - 1, 0.0, pltpu.roll(wide, count - 1, 0)).astype(flat.dtype)
    return left, flat, right


def fill_weights(blocks, weight, flip):
    ch = weight.shape[2]
    zero = jnp.zeros((ch, ch), weight.dtype)
    for j in range(3):
        for b in range(2):
            for k in range(2):
                for n in range(2):
                    tap = 2 * b + k - n
                    ok = 0 <= tap <= 2
                    if flip:
                        value = weight[2 - tap, 2 - j] if ok else zero
                        blocks[j, b, n * ch : (n + 1) * ch, k * ch : (k + 1) * ch] = value
                    else:
                        value = weight[tap, j] if ok else zero
                        blocks[j, b, k * ch : (k + 1) * ch, n * ch : (n + 1) * ch] = value


def conv_pairs(taps, blocks, rows_out, cols, flip):
    dims = (((1,), (1,)), ((), ())) if flip else (((1,), (0,)), ((), ()))
    total = None
    for j in range(3):
        for b in range(2):
            part = lax.dot_general(
                taps[j][b * cols : b * cols + rows_out],
                blocks[j, b],
                dims,
                preferred_element_type=F32,
            )
            total = part if total is None else total + part
    return total


def drive_kernel(field, top, bottom, weight, rate, local, end, taps_out, pairs, blocks, *, flip):
    times, rows, cols, ch = field.shape
    half = rows // 2
    fill_weights(blocks, weight, flip)
    fill_pairs(pairs, field, top, bottom)
    carry = None
    for step in range(times):
        t = times - 1 - step if flip else step
        taps = column_taps(pairs[t].reshape((half + 1) * cols, 2 * ch), cols)
        for j in range(3):
            taps_out[j, t] = taps[j]
        value = conv_pairs(taps, blocks, half * cols, cols, flip)
        d = rate[t : t + 1, :]
        if flip:
            value = value if carry is None else value + carry
            carry = d * value
        else:
            value = (1.0 - d) * value
            value = value if carry is None else d * carry + value
            carry = value
        local[t] = value
    end[...] = carry


def drive_call(field, top, bottom, weight, rate, flip):
    times, rows, cols, ch = field.shape
    half = rows // 2
    return pl.pallas_call(
        functools.partial(drive_kernel, flip=flip),
        out_shape=(
            jax.ShapeDtypeStruct((times, half * cols, 2 * ch), F32),
            jax.ShapeDtypeStruct((half * cols, 2 * ch), F32),
            jax.ShapeDtypeStruct((3, times, (half + 1) * cols, 2 * ch), BF16),
        ),
        scratch_shapes=[
            pltpu.VMEM((times, half + 1, cols, 2 * ch), BF16),
            pltpu.VMEM((3, 2, 2 * ch, 2 * ch), BF16),
        ],
        compiler_params=pltpu.CompilerParams(vmem_limit_bytes=VMEM_LIMIT),
        cost_estimate=pl.CostEstimate(
            flops=times * rows * cols * ch * ch * 24, bytes_accessed=6 << 20, transcendentals=0
        ),
        name="drive_adjoint" if flip else "drive_state",
    )(field, top, bottom, weight, rate)


def grads_kernel(local, incoming, reach, gain, taps, rounded, grads, *, flip):
    times, count, width = local.shape
    ch = width // 2
    cols = taps.shape[2] - count
    add = incoming[...]
    turned = []
    for t in range(times):
        value = local[t] + reach[t : t + 1, :] * add
        if not flip:
            value = gain[t : t + 1, :] * value
        value = value.astype(BF16)
        rounded[t] = value
        turned.append(value.T)
    for j in range(3):
        blocks = []
        for b in range(2):
            total = None
            for t in range(times):
                part = jnp.dot(
                    turned[t], taps[j, t, b * cols : b * cols + count], preferred_element_type=F32
                )
                total = part if total is None else total + part
            blocks.append(total)
        for tap in range(3):
            total = None
            for b in range(2):
                for c in range(2):
                    a = 2 * b + c - tap
                    if a in (0, 1):
                        part = blocks[b][a * ch : (a + 1) * ch, c * ch : (c + 1) * ch]
                        total = part if total is None else total + part
            if flip:
                grads[2 - tap, 2 - j] = total
            else:
                grads[tap, j] = total.T


def grads_call(local, incoming, reach, gain, taps, flip):
    times, count, width = local.shape
    ch = width // 2
    return pl.pallas_call(
        functools.partial(grads_kernel, flip=flip),
        out_shape=(
            jax.ShapeDtypeStruct((times, count, width), BF16),
            jax.ShapeDtypeStruct((3, 3, ch, ch), F32),
        ),
        compiler_params=pltpu.CompilerParams(vmem_limit_bytes=VMEM_LIMIT),
        cost_estimate=pl.CostEstimate(
            flops=times * count * ch * ch * 48, bytes_accessed=6 << 20, transcendentals=0
        ),
        name="grads_out" if flip else "grads_in",
    )(local, incoming, reach, gain, taps)


def output_kernel(field, top, bottom, weight, skip, direct, out, pairs, blocks, *, flip):
    times, half, cols, width = field.shape
    ch = width // 2
    fill_weights(blocks, weight, flip)
    fill_pairs_from_pairs(pairs, field, top, bottom)
    gain = skip[...]
    for t in range(times):
        taps = column_taps(pairs[t].reshape((half + 1) * cols, width), cols)
        value = conv_pairs(taps, blocks, half * cols, cols, flip).reshape(half, cols, width)
        for i in range(half):
            for c in range(2):
                base = gain * direct[t, 2 * i + c].astype(F32)
                out[t, 2 * i + c] = (value[i, :, c * ch : (c + 1) * ch] + base).astype(BF16)


def output_call(field, top, bottom, weight, skip, direct, flip):
    times, half, cols, width = field.shape
    ch = width // 2
    return pl.pallas_call(
        functools.partial(output_kernel, flip=flip),
        out_shape=jax.ShapeDtypeStruct(direct.shape, BF16),
        scratch_shapes=[
            pltpu.VMEM((times, half + 1, cols, width), BF16),
            pltpu.VMEM((3, 2, width, width), BF16),
        ],
        compiler_params=pltpu.CompilerParams(vmem_limit_bytes=VMEM_LIMIT),
        cost_estimate=pl.CostEstimate(
            flops=times * half * cols * ch * ch * 48, bytes_accessed=4 << 20, transcendentals=0
        ),
        name="grad_frames" if flip else "output",
    )(field, top, bottom, weight, skip, direct)


def neighbours(axis, low, high):
    count = lax.axis_size(axis)
    forward = [(i, i + 1) for i in range(count - 1)]
    backward = [(i + 1, i) for i in range(count - 1)]
    return lax.ppermute(low, axis, forward), lax.ppermute(high, axis, backward)


def swap(value, axis, bit):
    count = lax.axis_size(axis)
    return lax.ppermute(value, axis, [(i, i ^ bit) for i in range(count)])


def shift(value, axis, by):
    count = lax.axis_size(axis)
    return lax.ppermute(value, axis, [(i, i + by) for i in range(count) if 0 <= i + by < count])


def carry_over(end, total, axis, sign):
    count = lax.axis_size(axis)
    place = lax.axis_index(axis)
    odd = place % 2 == 1
    half = end.shape[0] // 2
    width = end.shape[1]

    def message(value, decay):
        return jnp.concatenate([value, jnp.broadcast_to(decay, (8, width))], 0)

    low, high = end[:half], end[half:]
    mine = jnp.where(odd, high, low)
    got = swap(message(jnp.where(odd, low, high), total), axis, 1)
    theirs, their_total = got[:half], got[half : half + 1]
    late = odd if sign > 0 else jnp.logical_not(odd)
    first = jnp.where(late, theirs, mine)
    first_total = jnp.where(late, their_total, total)
    second = jnp.where(late, mine, theirs)
    second_total = jnp.where(late, total, their_total)
    pair = second_total * first + second
    pair_total = first_total * second_total

    before = jnp.zeros_like(pair)
    before_total = jnp.ones_like(pair_total)
    reached = 1
    while reached < count // 2:
        upto = pair + pair_total * before
        got = shift(message(upto, pair_total * before_total), axis, 2 * reached * sign)
        before = before + before_total * got[:half]
        before_total = before_total * got[half : half + 1]
        reached *= 2
    inner = first + first_total * before
    own = jnp.where(late, inner, before)
    other = swap(jnp.where(late, before, inner), axis, 1)
    return jnp.concatenate([jnp.where(odd, other, own), jnp.where(odd, own, other)], 0)


def summed(in_part, out_part):
    ch_in, ch_out = in_part.shape[2:]
    core = lax.axis_index("tile") % 2 == 1
    flat_in = in_part.reshape(-1, ch_out)
    flat_out = out_part.reshape(-1, ch_out)
    got = swap(jnp.where(core, flat_in, flat_out), "tile", 1)
    value = jnp.where(core, flat_out, flat_in) + got
    steps = []
    bit = 1
    while bit < lax.axis_size("tm"):
        steps.append(("tm", bit))
        bit *= 2
    bit = 2
    while bit < lax.axis_size("tile"):
        steps.insert(1, ("tile", bit))
        bit *= 2
    for axis, bit in steps:
        half = value.shape[0] // 2
        high = (lax.axis_index(axis) // bit) % 2 == 1
        low_part, high_part = value[:half], value[half:]
        got = swap(jnp.where(high, low_part, high_part), axis, bit)
        value = jnp.where(high, high_part, low_part) + got
    for axis, bit in reversed(steps):
        high = (lax.axis_index(axis) // bit) % 2 == 1
        got = swap(value, axis, bit)
        value = jnp.concatenate([jnp.where(high, got, value), jnp.where(high, value, got)], 0)
    got = swap(value, "tile", 1)
    shape = in_part.shape
    return (
        jnp.where(core, got, value).reshape(shape),
        jnp.where(core, value, got).reshape(shape),
    )


def shards(frames, cotangent, w_in, w_out, skip, log_decay):
    times, rows, cols, ch = frames.shape
    half = rows // 2
    decay = jnp.exp(log_decay)
    wide = jnp.concatenate([decay, decay], 1)
    cumulative = jnp.cumsum(log_decay, axis=0)
    reach = jnp.exp(cumulative)
    tail = jnp.exp(cumulative[-1][None, :] - cumulative)
    reach = jnp.concatenate([reach, reach], 1)
    tail = jnp.concatenate([tail, tail], 1)
    total = reach[-1:]

    frames_top, frames_bottom = neighbours("tile", frames[:, -1:], frames[:, :1])
    cot_top, cot_bottom = neighbours("tile", cotangent[:, -1:], cotangent[:, :1])

    states, state_end, frame_taps = drive_call(
        frames, frames_top, frames_bottom, w_in, wide, False
    )
    adjoints, adjoint_end, cot_taps = drive_call(
        cotangent, cot_top, cot_bottom, w_out, wide, True
    )
    state_in = carry_over(state_end, total, "tm", 1)
    adjoint_in = carry_over(adjoint_end, total, "tm", -1)

    states_bf, out_part = grads_call(states, state_in, reach, reach, cot_taps, True)
    inflow_bf, in_part = grads_call(adjoints, adjoint_in, tail, 1.0 - wide, frame_taps, False)

    factor = 1.0 / math.sqrt(
        times * lax.axis_size("tm") * rows * lax.axis_size("tile") * cols
    )
    in_sum, out_sum = summed(in_part, out_part)

    states_bf = states_bf.reshape(times, half, cols, 2 * ch)
    inflow_bf = inflow_bf.reshape(times, half, cols, 2 * ch)
    gain = skip[None, :]
    states_top, states_bottom = neighbours(
        "tile", states_bf[:, -1:, :, ch:], states_bf[:, :1, :, :ch]
    )
    inflow_top, inflow_bottom = neighbours(
        "tile", inflow_bf[:, -1:, :, ch:], inflow_bf[:, :1, :, :ch]
    )
    output = output_call(states_bf, states_top, states_bottom, w_out, gain, frames, False)
    grad_frames = output_call(
        inflow_bf, inflow_top, inflow_bottom, w_in, gain, cotangent, True
    )
    return (output, grad_frames, in_sum * factor, out_sum * factor)


def solution(mesh):
    placed = (
        P("tm", "tile", None, None),
        P("tm", "tile", None, None),
        P(),
        P(),
        P(),
        P("tm", None),
    )
    return jax.shard_map(
        shards,
        mesh=mesh,
        in_specs=placed,
        out_specs=(P("tm", "tile", None, None), P("tm", "tile", None, None), P(), P()),
        check_vma=False,
    )
```

```python
import functools
import math

import jax
import jax.numpy as jnp
from jax import lax
from jax.experimental import pallas as pl
from jax.experimental.pallas import tpu as pltpu
from jax.sharding import PartitionSpec as P

F32 = jnp.float32
BF16 = jnp.bfloat16
VMEM_LIMIT = 40 * 1024 * 1024


def fill_pairs(pairs, field, top, bottom):
    half = field.shape[1] // 2
    ch = field.shape[3]
    pairs[:, 0, :, :ch] = top[:, 0]
    pairs[:, half, :, ch:] = bottom[:, 0]
    for i in range(half):
        pairs[:, i, :, ch:] = field[:, 2 * i]
        pairs[:, i + 1, :, :ch] = field[:, 2 * i + 1]


def fill_pairs_from_pairs(pairs, field, top, bottom):
    half = field.shape[1]
    ch = field.shape[3] // 2
    pairs[:, 0, :, :ch] = top[:, 0]
    pairs[:, half, :, ch:] = bottom[:, 0]
    pairs[:, :half, :, ch:] = field[:, :, :, :ch]
    pairs[:, 1:, :, :ch] = field[:, :, :, ch:]


def column_taps(flat, cols):
    wide = flat.astype(F32)
    count = wide.shape[0]
    col = lax.broadcasted_iota(jnp.int32, wide.shape, 0) % cols
    left = jnp.where(col == 0, 0.0, pltpu.roll(wide, 1, 0)).astype(flat.dtype)
    right = jnp.where(col == cols - 1, 0.0, pltpu.roll(wide, count - 1, 0)).astype(flat.dtype)
    return left, flat, right


def fill_weights(blocks, weight, flip):
    ch = weight.shape[2]
    zero = jnp.zeros((ch, ch), weight.dtype)
    for j in range(3):
        for b in range(2):
            for k in range(2):
                for n in range(2):
                    tap = 2 * b + k - n
                    ok = 0 <= tap <= 2
                    if flip:
                        value = weight[2 - tap, 2 - j] if ok else zero
                        blocks[j, b, n * ch : (n + 1) * ch, k * ch : (k + 1) * ch] = value
                    else:
                        value = weight[tap, j] if ok else zero
                        blocks[j, b, k * ch : (k + 1) * ch, n * ch : (n + 1) * ch] = value


def conv_pairs(taps, blocks, rows_out, cols, flip):
    dims = (((1,), (1,)), ((), ())) if flip else (((1,), (0,)), ((), ()))
    total = None
    for j in range(3):
        for b in range(2):
            part = lax.dot_general(
                taps[j][b * cols : b * cols + rows_out],
                blocks[j, b],
                dims,
                preferred_element_type=F32,
            )
            total = part if total is None else total + part
    return total


def pick_halos(first, second, index, odd, times):
    one = first[index].astype(F32)
    two = second[index].astype(F32)
    upper = jnp.where(odd, one, two).astype(BF16)
    lower = jnp.where(odd, two, one).astype(BF16)
    return upper[:, None], lower[:, None]


def exponent(value):
    top = jnp.max(jnp.abs(value), axis=0, keepdims=True)
    return jnp.ceil(jnp.log2(jnp.maximum(top, 1e-30)))


def decays(log_decay):
    wide = jnp.concatenate([log_decay, log_decay], 1)
    times = wide.shape[0]
    sums = [wide[0:1]]
    for t in range(1, times):
        sums.append(sums[-1] + wide[t : t + 1])
    rate = [jnp.exp(wide[t : t + 1]) for t in range(times)]
    reach = [jnp.exp(total) for total in sums]
    tail = [jnp.exp(sums[-1] - total) for total in sums]
    return rate, reach, tail


def drive_kernel(
    parity,
    frames,
    cotangent,
    first,
    second,
    w_in,
    w_out,
    log_decay,
    states,
    adjoints,
    leaving,
    frame_taps,
    cot_taps,
    info,
    pairs,
    blocks,
):
    times, rows, cols, ch = frames.shape
    half = rows // 2
    odd = parity[0] == 1
    rate, reach, _ = decays(log_decay[...])
    fields = ((frames, w_in, states, frame_taps), (cotangent, w_out, adjoints, cot_taps))
    for index, (field, weight, result, taps_out) in enumerate(fields):
        flip = index == 1
        top, bottom = pick_halos(first, second, index, odd, times)
        fill_weights(blocks.at[index], weight, flip)
        fill_pairs(pairs.at[index], field, top, bottom)
        carry = None
        for step in range(times):
            t = times - 1 - step if flip else step
            taps = column_taps(pairs[index, t].reshape((half + 1) * cols, 2 * ch), cols)
            for j in range(3):
                taps_out[j, t] = taps[j]
            value = conv_pairs(taps, blocks.at[index], half * cols, cols, flip)
            if flip:
                value = value if carry is None else value + carry
                carry = rate[t] * value
            else:
                value = (1.0 - rate[t]) * value
                value = value if carry is None else rate[t] * carry + value
                carry = value
            result[t] = value
        if flip:
            leaving[...] = carry
        info[index : index + 1, :] = exponent(carry)
    total = reach[-1]
    high = total.astype(BF16).astype(F32)
    rest = (total - high) * 256.0
    middle = rest.astype(BF16).astype(F32)
    low = ((rest - middle) * 256.0).astype(BF16).astype(F32)
    info[2:3, :] = high
    info[3:4, :] = middle
    info[4:5, :] = low
    info[5:, :] = jnp.zeros((info.shape[0] - 5, 2 * ch), F32)


def drive_call(parity, frames, cotangent, first, second, w_in, w_out, log_decay):
    times, rows, cols, ch = frames.shape
    half = rows // 2
    field = jax.ShapeDtypeStruct((times, half * cols, 2 * ch), F32)
    taps = jax.ShapeDtypeStruct((3, times, (half + 1) * cols, 2 * ch), BF16)
    return pl.pallas_call(
        drive_kernel,
        in_specs=[pl.BlockSpec(memory_space=pltpu.SMEM)]
        + [pl.BlockSpec(memory_space=pltpu.VMEM)] * 7,
        out_shape=(
            field,
            field,
            jax.ShapeDtypeStruct(field.shape[1:], F32),
            taps,
            taps,
            jax.ShapeDtypeStruct((16, 2 * ch), F32),
        ),
        scratch_shapes=[
            pltpu.VMEM((2, times, half + 1, cols, 2 * ch), BF16),
            pltpu.VMEM((2, 3, 2, 2 * ch, 2 * ch), BF16),
        ],
        compiler_params=pltpu.CompilerParams(vmem_limit_bytes=VMEM_LIMIT),
        cost_estimate=pl.CostEstimate(
            flops=times * rows * cols * ch * ch * 48, bytes_accessed=12 << 20, transcendentals=0
        ),
        name="drive",
    )(parity, frames, cotangent, first, second, w_in, w_out, log_decay)


def grads_kernel(
    parity,
    states,
    adjoints,
    state_in,
    adjoint_in,
    log_decay,
    frame_taps,
    cot_taps,
    states_bf,
    inflow_bf,
    first,
    second,
    grads_in,
    grads_out,
    info,
    turned,
):
    times, count, width = states.shape
    ch = width // 2
    cols = frame_taps.shape[2] - count
    odd = parity[0] == 1
    rate, reach, tail = decays(log_decay[...])
    add = state_in[...]
    back = adjoint_in[...]
    for t in range(times):
        value = (states[t] + reach[t] * add).astype(BF16)
        states_bf[t] = value
        turned[0, t] = value.T
        value = ((1.0 - rate[t]) * (adjoints[t] + tail[t] * back)).astype(BF16)
        inflow_bf[t] = value
        turned[1, t] = value.T
        for index, field in enumerate((states_bf, inflow_bf)):
            low = field[t, :cols, :ch].astype(F32)
            high = field[t, count - cols :, ch:].astype(F32)
            first[index, t] = jnp.where(odd, low, high).astype(BF16)
            second[index, t] = jnp.where(odd, high, low).astype(BF16)
    for index, (taps, grads) in enumerate(((cot_taps, grads_out), (frame_taps, grads_in))):
        largest = None
        for j in range(3):
            blocks = []
            for b in range(2):
                total = None
                for t in range(times):
                    part = jnp.dot(
                        turned[index, t],
                        taps[j, t, b * cols : b * cols + count],
                        preferred_element_type=F32,
                    )
                    total = part if total is None else total + part
                blocks.append(total)
            for tap in range(3):
                total = None
                for b in range(2):
                    for c in range(2):
                        a = 2 * b + c - tap
                        if a in (0, 1):
                            part = blocks[b][a * ch : (a + 1) * ch, c * ch : (c + 1) * ch]
                            total = part if total is None else total + part
                if index == 0:
                    place = (2 - tap) * 3 + 2 - j
                else:
                    place = tap * 3 + j
                    total = total.T
                grads[place * ch : (place + 1) * ch, :] = total
                top = jnp.max(jnp.abs(total), axis=0, keepdims=True)
                largest = top if largest is None else jnp.maximum(largest, top)
        info[index * 8 : index * 8 + 8, :] = jnp.broadcast_to(exponent(largest), (8, ch))


def grads_call(parity, states, adjoints, state_in, adjoint_in, log_decay, frame_taps, cot_taps):
    times, count, width = states.shape
    ch = width // 2
    cols = frame_taps.shape[2] - count
    field = jax.ShapeDtypeStruct((times, count, width), BF16)
    edge = jax.ShapeDtypeStruct((2, times, cols, ch), BF16)
    grads = jax.ShapeDtypeStruct((9 * ch, ch), F32)
    return pl.pallas_call(
        grads_kernel,
        in_specs=[pl.BlockSpec(memory_space=pltpu.SMEM)]
        + [pl.BlockSpec(memory_space=pltpu.VMEM)] * 7,
        out_shape=(field, field, edge, edge, grads, grads, jax.ShapeDtypeStruct((16, ch), F32)),
        scratch_shapes=[pltpu.VMEM((2, times, width, count), BF16)],
        compiler_params=pltpu.CompilerParams(vmem_limit_bytes=VMEM_LIMIT),
        cost_estimate=pl.CostEstimate(
            flops=times * count * ch * ch * 96, bytes_accessed=12 << 20, transcendentals=0
        ),
        name="grads",
    )(parity, states, adjoints, state_in, adjoint_in, log_decay, frame_taps, cot_taps)


def output_kernel(parity, field, first, second, weight, skip, direct, out, pairs, blocks, *, flip):
    times, half, cols, width = field.shape
    ch = width // 2
    fill_weights(blocks, weight, flip)
    top, bottom = pick_halos(first, second, int(flip), parity[0] == 1, times)
    fill_pairs_from_pairs(pairs, field, top, bottom)
    gain = skip[...]
    for t in range(times):
        taps = column_taps(pairs[t].reshape((half + 1) * cols, width), cols)
        value = conv_pairs(taps, blocks, half * cols, cols, flip).reshape(half, cols, width)
        for i in range(half):
            for c in range(2):
                base = gain * direct[t, 2 * i + c].astype(F32)
                out[t, 2 * i + c] = (value[i, :, c * ch : (c + 1) * ch] + base).astype(BF16)


def output_call(parity, field, first, second, weight, skip, direct, flip):
    times, half, cols, width = field.shape
    ch = width // 2
    return pl.pallas_call(
        functools.partial(output_kernel, flip=flip),
        in_specs=[pl.BlockSpec(memory_space=pltpu.SMEM)]
        + [pl.BlockSpec(memory_space=pltpu.VMEM)] * 6,
        out_shape=jax.ShapeDtypeStruct(direct.shape, BF16),
        scratch_shapes=[
            pltpu.VMEM((times, half + 1, cols, width), BF16),
            pltpu.VMEM((3, 2, width, width), BF16),
        ],
        compiler_params=pltpu.CompilerParams(vmem_limit_bytes=VMEM_LIMIT),
        cost_estimate=pl.CostEstimate(
            flops=times * half * cols * ch * ch * 48, bytes_accessed=4 << 20, transcendentals=0
        ),
        name="grad_frames" if flip else "output",
    )(parity, field, first, second, weight, skip, direct)


def swap(value, tm_bits, tile_bits):
    tiles = lax.axis_size("tile")
    mask = tm_bits * tiles + tile_bits
    count = lax.axis_size("tm") * tiles
    return lax.ppermute(value, ("tm", "tile"), [(i, i ^ mask) for i in range(count)])


def swap_across(value):
    count = lax.axis_size("tile")
    pairs = []
    for i in range(1, count - 1, 2):
        pairs += [(i, i + 1), (i + 1, i)]
    return lax.ppermute(value, "tile", pairs)


def packed(value, scale, rows):
    pad = jnp.zeros((16 - rows.shape[0], rows.shape[1]), F32)
    return jnp.concatenate([value * jnp.exp2(-scale), rows, pad], 0).astype(jnp.float16)


def whole_decay(rows):
    return rows[0:1] + rows[1:2] / 256.0 + rows[2:3] / 65536.0


def carry_over(state_end, adjoint_end, info):
    count = lax.axis_size("tm")
    place = lax.axis_index("tm")
    odd = place % 2 == 1
    pair_place = place // 2
    half = state_end.shape[0] // 2

    def both(low, high, scale_low, scale_high, rows):
        pad = jnp.zeros((16 - rows.shape[0], rows.shape[1]), F32)
        return jnp.concatenate(
            [low * jnp.exp2(-scale_low), high * jnp.exp2(-scale_high), rows, pad], 0
        ).astype(jnp.float16)

    def give(value, mine):
        return jnp.where(odd == mine, value[half:], value[:half])

    got = swap(
        both(give(state_end, False), give(adjoint_end, False), info[0:1], info[1:2], info[:5]), 1, 0
    ).astype(F32)
    their_info = got[2 * half : 2 * half + 5]
    total, their_total = whole_decay(info[2:5]), whole_decay(their_info[2:5])
    even_total = jnp.where(odd, their_total, total)
    odd_total = jnp.where(odd, total, their_total)
    state_mine, adjoint_mine = give(state_end, True), give(adjoint_end, True)
    state_theirs = got[:half] * jnp.exp2(their_info[0:1])
    adjoint_theirs = got[half : 2 * half] * jnp.exp2(their_info[1:2])
    state_even = jnp.where(odd, state_theirs, state_mine)
    state_odd = jnp.where(odd, state_mine, state_theirs)
    adjoint_even = jnp.where(odd, adjoint_theirs, adjoint_mine)
    adjoint_odd = jnp.where(odd, adjoint_mine, adjoint_theirs)
    state_pair = odd_total * state_even + state_odd
    adjoint_pair = adjoint_even + even_total * adjoint_odd
    state_scale = jnp.maximum(info[0:1], their_info[0:1])
    adjoint_scale = jnp.maximum(info[1:2], their_info[1:2])

    messages = []
    bit = 1
    while bit < count // 2:
        later = (pair_place // bit) % 2 == 1
        scale = jnp.where(later, adjoint_scale, state_scale)
        rows = jnp.concatenate([scale, info[2:5], their_info[2:5]], 0)
        messages.append(packed(jnp.where(later, adjoint_pair, state_pair), scale, rows))
        bit *= 2
    received = {}
    for d in range(1, count // 2):
        received[d] = swap(messages[d.bit_length() - 1], 2 * d, 0).astype(F32)
    totals, values = {}, {}
    top_scale = jnp.maximum(state_scale, adjoint_scale)
    for d, got in received.items():
        rows = got[half : half + 7]
        totals[d] = whole_decay(rows[1:4]) * whole_decay(rows[4:7])
        values[d] = got[:half] * jnp.exp2(rows[0:1])
        top_scale = jnp.maximum(top_scale, rows[0:1])
    state_before = jnp.zeros_like(state_pair)
    adjoint_after = jnp.zeros_like(adjoint_pair)
    for d in received:
        other = pair_place ^ d
        through = jnp.ones_like(top_scale)
        for e in received:
            between = pair_place ^ e
            inside = ((other < between) & (between < pair_place)) | (
                (pair_place < between) & (between < other)
            )
            through = through * jnp.where(inside, totals[e], 1.0)
        term = through * values[d]
        state_before = state_before + jnp.where(other < pair_place, term, 0.0)
        adjoint_after = adjoint_after + jnp.where(other > pair_place, term, 0.0)

    state_inner = state_even + even_total * state_before
    adjoint_inner = adjoint_odd + odd_total * adjoint_after
    state_keep = jnp.where(odd, state_inner, state_before)
    state_send = jnp.where(odd, state_before, state_inner)
    adjoint_keep = jnp.where(odd, adjoint_after, adjoint_inner)
    adjoint_send = jnp.where(odd, adjoint_inner, adjoint_after)
    got = swap(both(state_send, adjoint_send, top_scale, top_scale, top_scale), 1, 0).astype(F32)
    scale = jnp.exp2(got[2 * half : 2 * half + 1])

    def joined(keep, other):
        return jnp.concatenate([jnp.where(odd, other, keep), jnp.where(odd, keep, other)], 0)

    return (
        joined(state_keep, got[:half] * scale),
        joined(adjoint_keep, got[half : 2 * half] * scale),
    )


def unpacked(got):
    rows = got.shape[-2] - 16
    wide = got.astype(F32)
    scale = wide[..., rows : rows + 1, :]
    return wide[..., :rows, :] * jnp.exp2(scale), scale


def bit_set(tm_bits, tile_bits):
    place = lax.axis_index("tm") // tm_bits if tm_bits else lax.axis_index("tile") // tile_bits
    return place % 2 == 1


def shards(frames, cotangent, w_in, w_out, skip, log_decay):
    times, rows, cols, ch = frames.shape
    half = rows // 2
    tile = lax.axis_index("tile")
    odd = tile % 2 == 1
    parity = (tile % 2).reshape(1).astype(jnp.int32)
    gain = skip[None, :]

    low = jnp.stack([frames[:, 0], cotangent[:, 0]])
    high = jnp.stack([frames[:, -1], cotangent[:, -1]])
    second = swap_across(jnp.where(odd, high, low))
    first = swap(jnp.where(odd, low, high), 0, 1)

    states, adjoints, leaving, frame_taps, cot_taps, info = drive_call(
        parity, frames, cotangent, first, second, w_in, w_out, log_decay
    )
    state_in, adjoint_in = carry_over(states[-1], leaving, info)
    states_bf, inflow_bf, first, second, in_part, out_part, info = grads_call(
        parity, states, adjoints, state_in, adjoint_in, log_decay, frame_taps, cot_taps
    )

    in_scale, out_scale = info[8:9], info[0:1]
    scale = jnp.where(odd, in_scale, out_scale)
    message = packed(jnp.where(odd, in_part, out_part), scale, scale)
    message, first, second = lax.optimization_barrier((message, first, second))
    got, got_scale = unpacked(swap(message, 0, 1))
    value = jnp.where(odd, out_part, in_part) + got
    scale = jnp.maximum(jnp.where(odd, out_scale, in_scale), got_scale)
    second = swap_across(second)
    first = swap(first, 0, 1)

    bits = [(1, 0), (0, 2)] if lax.axis_size("tile") > 2 else [(1, 0)]
    parts = 2 ** len(bits)
    place = sum(bit_set(*bit).astype(jnp.int32) * 2**n for n, bit in enumerate(bits))
    pieces = value.reshape(parts, -1, ch)

    def mask(d):
        chosen = [bit for n, bit in enumerate(bits) if d >> n & 1]
        return sum(b[0] for b in chosen), sum(b[1] for b in chosen)

    messages = [
        packed(lax.dynamic_index_in_dim(pieces, place ^ d, 0, False), scale, scale)
        for d in range(1, parts)
    ]
    value = lax.dynamic_index_in_dim(pieces, place, 0, False)
    states_bf = states_bf.reshape(times, half, cols, 2 * ch)
    inflow_bf = inflow_bf.reshape(times, half, cols, 2 * ch)
    *messages, states_bf = lax.optimization_barrier((*messages, states_bf))
    received = [swap(m, *mask(d + 1)) for d, m in enumerate(messages)]
    output = output_call(parity, states_bf, first, second, w_out, gain, frames, False)
    for got in received:
        got, got_scale = unpacked(got)
        value = value + got
        scale = jnp.maximum(scale, got_scale)

    left = []
    bit = 2
    while bit < lax.axis_size("tm"):
        left.append((bit, 0))
        bit *= 2
    bit = 4
    while bit < lax.axis_size("tile"):
        left.append((0, bit))
        bit *= 2
    waiting = inflow_bf
    for n in range(0, len(left), 2):
        group = left[n : n + 2]
        message = packed(value, scale, scale)
        message, output, waiting = lax.optimization_barrier((message, output, waiting))
        terms = [message]
        for d in range(1, 2 ** len(group)):
            chosen = [b for k, b in enumerate(group) if d >> k & 1]
            terms.append(swap(message, sum(b[0] for b in chosen), sum(b[1] for b in chosen)))
        terms = [unpacked(term) for term in terms]
        while len(terms) > 1:
            terms = [
                (a[0] + b[0], jnp.maximum(a[1], b[1])) for a, b in zip(terms[::2], terms[1::2])
            ]
        value, scale = terms[0]
    grad_frames = output_call(parity, waiting, first, second, w_in, gain, cotangent, True)

    message = packed(value, scale, scale)
    message, grad_frames = lax.optimization_barrier((message, grad_frames))
    gathered = [message] + [swap(message, *mask(d)) for d in range(1, parts)]
    for bit in bits:
        high = bit_set(*bit)
        gathered = [
            (jnp.where(high, b, a), jnp.where(high, a, b))
            for a, b in zip(gathered[::2], gathered[1::2])
        ]
        gathered = [jnp.concatenate(pair, 0) for pair in gathered]
    (mine,) = gathered
    mine = lax.optimization_barrier(mine)
    theirs = swap(mine, 0, 1)
    factor = 1.0 / math.sqrt(
        times * lax.axis_size("tm") * rows * lax.axis_size("tile") * cols
    )
    results = []
    for chosen in (jnp.where(odd, theirs, mine), jnp.where(odd, mine, theirs)):
        whole, _ = unpacked(chosen.reshape(parts, -1, ch))
        results.append((whole * factor).reshape(3, 3, ch, ch))
    return (output, grad_frames, results[0], results[1])


def solution(mesh):
    placed = (
        P("tm", "tile", None, None),
        P("tm", "tile", None, None),
        P(),
        P(),
        P(),
        P("tm", None),
    )
    return jax.shard_map(
        shards,
        mesh=mesh,
        in_specs=placed,
        out_specs=(P("tm", "tile", None, None), P("tm", "tile", None, None), P(), P()),
        check_vma=False,
    )
```

```python
import functools
import math

import jax
import jax.numpy as jnp
from jax import lax
from jax.experimental import pallas as pl
from jax.experimental.pallas import tpu as pltpu
from jax.sharding import PartitionSpec as P

F32 = jnp.float32
BF16 = jnp.bfloat16
VMEM_LIMIT = 24 * 1024 * 1024


def fill_pairs(pairs, field, top, bottom):
    half = field.shape[1] // 2
    ch = field.shape[3]
    pairs[:, 0, :, :ch] = top[:, 0]
    pairs[:, half, :, ch:] = bottom[:, 0]
    for i in range(half):
        pairs[:, i, :, ch:] = field[:, 2 * i]
        pairs[:, i + 1, :, :ch] = field[:, 2 * i + 1]


def fill_pairs_from_pairs(pairs, field, top, bottom):
    half = field.shape[1]
    ch = field.shape[3] // 2
    pairs[:, 0, :, :ch] = top[:, 0]
    pairs[:, half, :, ch:] = bottom[:, 0]
    pairs[:, :half, :, ch:] = field[:, :, :, :ch]
    pairs[:, 1:, :, :ch] = field[:, :, :, ch:]


def column_taps(flat, cols):
    wide = flat.astype(F32)
    count = wide.shape[0]
    col = lax.broadcasted_iota(jnp.int32, wide.shape, 0) % cols
    left = jnp.where(col == 0, 0.0, pltpu.roll(wide, 1, 0)).astype(flat.dtype)
    right = jnp.where(col == cols - 1, 0.0, pltpu.roll(wide, count - 1, 0)).astype(flat.dtype)
    return left, flat, right


def fill_weights(blocks, weight, flip):
    ch = weight.shape[2]
    zero = jnp.zeros((ch, ch), weight.dtype)
    for j in range(3):
        for b in range(2):
            for k in range(2):
                for n in range(2):
                    tap = 2 * b + k - n
                    ok = 0 <= tap <= 2
                    if flip:
                        value = weight[2 - tap, 2 - j] if ok else zero
                        blocks[j, b, n * ch : (n + 1) * ch, k * ch : (k + 1) * ch] = value
                    else:
                        value = weight[tap, j] if ok else zero
                        blocks[j, b, k * ch : (k + 1) * ch, n * ch : (n + 1) * ch] = value


def conv_pairs(taps, blocks, rows_out, cols, flip):
    dims = (((1,), (1,)), ((), ())) if flip else (((1,), (0,)), ((), ()))
    total = None
    for j in range(3):
        for b in range(2):
            part = lax.dot_general(
                taps[j][b * cols : b * cols + rows_out],
                blocks[j, b],
                dims,
                preferred_element_type=F32,
            )
            total = part if total is None else total + part
    return total


def pick_halos(first, second, index, odd, times):
    one = first[index].astype(F32)
    two = second[index].astype(F32)
    upper = jnp.where(odd, one, two).astype(BF16)
    lower = jnp.where(odd, two, one).astype(BF16)
    return upper[:, None], lower[:, None]


def exponent(value):
    top = jnp.max(jnp.abs(value), axis=0, keepdims=True)
    return jnp.ceil(jnp.log2(jnp.maximum(top, 1e-30)))


def decays(log_decay):
    wide = jnp.concatenate([log_decay, log_decay], 1)
    times = wide.shape[0]
    sums = [wide[0:1]]
    for t in range(1, times):
        sums.append(sums[-1] + wide[t : t + 1])
    rate = [jnp.exp(wide[t : t + 1]) for t in range(times)]
    reach = [jnp.exp(total) for total in sums]
    tail = [jnp.exp(sums[-1] - total) for total in sums]
    return rate, reach, tail


def blocks_kernel(frames, cotangent, w_in, w_out, log_decay, blocks):
    fill_weights(blocks.at[0], w_in, False)
    fill_weights(blocks.at[1], w_out, True)


def blocks_call(frames, cotangent, w_in, w_out, log_decay):
    ch = w_in.shape[2]
    return pl.pallas_call(
        blocks_kernel,
        out_shape=jax.ShapeDtypeStruct((2, 3, 2, 2 * ch, 2 * ch), BF16),
        compiler_params=pltpu.CompilerParams(vmem_limit_bytes=VMEM_LIMIT),
        cost_estimate=pl.CostEstimate(flops=0, bytes_accessed=10 << 20, transcendentals=0),
        name="blocks",
    )(frames, cotangent, w_in, w_out, log_decay)


def drive_kernel(
    place,
    frames,
    cotangent,
    first,
    second,
    blocks,
    log_decay,
    states,
    adjoints,
    leaving,
    frame_taps,
    cot_taps,
    info,
    pairs,
):
    times, rows, cols, ch = frames.shape
    half = rows // 2
    odd = lax.rem(place[0], 2) == 1
    rate, reach, _ = decays(log_decay[...])
    fields = ((frames, states, frame_taps), (cotangent, adjoints, cot_taps))
    for index, (field, result, taps_out) in enumerate(fields):
        flip = index == 1
        top, bottom = pick_halos(first, second, index, odd, times)
        fill_pairs(pairs.at[index], field, top, bottom)
        carry = None
        for step in range(times):
            t = times - 1 - step if flip else step
            taps = column_taps(pairs[index, t].reshape((half + 1) * cols, 2 * ch), cols)
            for j in range(3):
                taps_out[j, t] = taps[j]
            value = conv_pairs(taps, blocks.at[index], half * cols, cols, flip)
            if flip:
                value = value if carry is None else value + carry
                carry = rate[t] * value
            else:
                value = (1.0 - rate[t]) * value
                value = value if carry is None else rate[t] * carry + value
                carry = value
            result[t] = value
        if flip:
            leaving[...] = carry
        info[index : index + 1, :] = exponent(carry)
    total = reach[-1]
    high = total.astype(BF16).astype(F32)
    rest = (total - high) * 256.0
    middle = rest.astype(BF16).astype(F32)
    low = ((rest - middle) * 256.0).astype(BF16).astype(F32)
    info[2:3, :] = high
    info[3:4, :] = middle
    info[4:5, :] = low
    row = jnp.zeros((1, 2 * ch), F32)
    info[5:6, :] = row + lax.rem(place[1], 2).astype(F32)
    for d in range(info.shape[0] - 6):
        info[6 + d : 7 + d, :] = row + (lax.div(place[1], 2) ^ d).astype(F32)


def drive_call(place, frames, cotangent, first, second, blocks, log_decay):
    times, rows, cols, ch = frames.shape
    half = rows // 2
    field = jax.ShapeDtypeStruct((times, half * cols, 2 * ch), F32)
    rows_info = (6 + lax.axis_size("tm") // 2 + 15) // 16 * 16
    taps = jax.ShapeDtypeStruct((3, times, (half + 1) * cols, 2 * ch), BF16)
    return pl.pallas_call(
        drive_kernel,
        in_specs=[pl.BlockSpec(memory_space=pltpu.SMEM)]
        + [pl.BlockSpec(memory_space=pltpu.VMEM)] * 6,
        out_shape=(
            field,
            field,
            jax.ShapeDtypeStruct(field.shape[1:], F32),
            taps,
            taps,
            jax.ShapeDtypeStruct((rows_info, 2 * ch), F32),
        ),
        scratch_shapes=[
            pltpu.VMEM((2, times, half + 1, cols, 2 * ch), BF16),
        ],
        compiler_params=pltpu.CompilerParams(vmem_limit_bytes=VMEM_LIMIT),
        cost_estimate=pl.CostEstimate(
            flops=times * rows * cols * ch * ch * 48, bytes_accessed=12 << 20, transcendentals=0
        ),
        name="drive",
    )(place, frames, cotangent, first, second, blocks, log_decay)


def grads_kernel(
    place,
    states,
    adjoints,
    state_in,
    adjoint_in,
    log_decay,
    frame_taps,
    cot_taps,
    states_bf,
    inflow_bf,
    first,
    second,
    grads_in,
    grads_out,
    info,
    turned,
):
    times, count, width = states.shape
    ch = width // 2
    cols = frame_taps.shape[2] - count
    odd = lax.rem(place[0], 2) == 1
    rate, reach, tail = decays(log_decay[...])
    add = state_in[...]
    back = adjoint_in[...]
    for t in range(times):
        value = (states[t] + reach[t] * add).astype(BF16)
        states_bf[t] = value
        turned[0, t] = value.T
        value = ((1.0 - rate[t]) * (adjoints[t] + tail[t] * back)).astype(BF16)
        inflow_bf[t] = value
        turned[1, t] = value.T
        for index, field in enumerate((states_bf, inflow_bf)):
            low = field[t, :cols, :ch].astype(F32)
            high = field[t, count - cols :, ch:].astype(F32)
            first[index, t] = jnp.where(odd, low, high).astype(BF16)
            second[index, t] = jnp.where(odd, high, low).astype(BF16)
    for index, (taps, grads) in enumerate(((cot_taps, grads_out), (frame_taps, grads_in))):
        largest = None
        for j in range(3):
            blocks = []
            for b in range(2):
                total = None
                for t in range(times):
                    part = jnp.dot(
                        turned[index, t],
                        taps[j, t, b * cols : b * cols + count],
                        preferred_element_type=F32,
                    )
                    total = part if total is None else total + part
                blocks.append(total)
            for tap in range(3):
                total = None
                for b in range(2):
                    for c in range(2):
                        a = 2 * b + c - tap
                        if a in (0, 1):
                            part = blocks[b][a * ch : (a + 1) * ch, c * ch : (c + 1) * ch]
                            total = part if total is None else total + part
                if index == 0:
                    spot = (2 - tap) * 3 + 2 - j
                else:
                    spot = tap * 3 + j
                    total = total.T
                grads[spot * ch : (spot + 1) * ch, :] = total
                top = jnp.max(jnp.abs(total), axis=0, keepdims=True)
                largest = top if largest is None else jnp.maximum(largest, top)
        info[index : index + 1, :] = exponent(largest)
    row = jnp.zeros((1, ch), F32)
    info[2:3, :] = row + lax.rem(place[0], 2).astype(F32)
    info[3:4, :] = row + lax.rem(place[1], 2).astype(F32)
    info[4:5, :] = row + lax.rem(lax.div(place[0], 2), 2).astype(F32)
    info[5:, :] = jnp.zeros((info.shape[0] - 5, ch), F32)


def grads_call(place, states, adjoints, state_in, adjoint_in, log_decay, frame_taps, cot_taps):
    times, count, width = states.shape
    ch = width // 2
    cols = frame_taps.shape[2] - count
    field = jax.ShapeDtypeStruct((times, count, width), BF16)
    edge = jax.ShapeDtypeStruct((2, times, cols, ch), BF16)
    grads = jax.ShapeDtypeStruct((9 * ch, ch), F32)
    return pl.pallas_call(
        grads_kernel,
        in_specs=[pl.BlockSpec(memory_space=pltpu.SMEM)]
        + [pl.BlockSpec(memory_space=pltpu.VMEM)] * 7,
        out_shape=(field, field, edge, edge, grads, grads, jax.ShapeDtypeStruct((16, ch), F32)),
        scratch_shapes=[pltpu.VMEM((2, times, width, count), BF16)],
        compiler_params=pltpu.CompilerParams(vmem_limit_bytes=VMEM_LIMIT),
        cost_estimate=pl.CostEstimate(
            flops=times * count * ch * ch * 96, bytes_accessed=12 << 20, transcendentals=0
        ),
        name="grads",
    )(place, states, adjoints, state_in, adjoint_in, log_decay, frame_taps, cot_taps)


def output_kernel(place, field, first, second, weight, skip, direct, out, pairs, blocks, *, flip):
    times, half, cols, width = field.shape
    ch = width // 2
    fill_weights(blocks, weight, flip)
    top, bottom = pick_halos(first, second, int(flip), lax.rem(place[0], 2) == 1, times)
    fill_pairs_from_pairs(pairs, field, top, bottom)
    gain = skip[...]
    for t in range(times):
        taps = column_taps(pairs[t].reshape((half + 1) * cols, width), cols)
        value = conv_pairs(taps, blocks, half * cols, cols, flip).reshape(half, cols, width)
        for i in range(half):
            for c in range(2):
                base = gain * direct[t, 2 * i + c].astype(F32)
                out[t, 2 * i + c] = (value[i, :, c * ch : (c + 1) * ch] + base).astype(BF16)


def output_call(place, field, first, second, weight, skip, direct, flip):
    times, half, cols, width = field.shape
    ch = width // 2
    return pl.pallas_call(
        functools.partial(output_kernel, flip=flip),
        in_specs=[pl.BlockSpec(memory_space=pltpu.SMEM)]
        + [pl.BlockSpec(memory_space=pltpu.VMEM)] * 6,
        out_shape=jax.ShapeDtypeStruct(direct.shape, BF16),
        scratch_shapes=[
            pltpu.VMEM((times, half + 1, cols, width), BF16),
            pltpu.VMEM((3, 2, width, width), BF16),
        ],
        compiler_params=pltpu.CompilerParams(vmem_limit_bytes=VMEM_LIMIT),
        cost_estimate=pl.CostEstimate(
            flops=times * half * cols * ch * ch * 48, bytes_accessed=4 << 20, transcendentals=0
        ),
        name="grad_frames" if flip else "output",
    )(place, field, first, second, weight, skip, direct)


def swap(value, tm_bits, tile_bits):
    tiles = lax.axis_size("tile")
    mask = tm_bits * tiles + tile_bits
    count = lax.axis_size("tm") * tiles
    return lax.ppermute(value, ("tm", "tile"), [(i, i ^ mask) for i in range(count)])


def swap_across(value):
    count = lax.axis_size("tile")
    pairs = []
    for i in range(1, count - 1, 2):
        pairs += [(i, i + 1), (i + 1, i)]
    return lax.ppermute(value, "tile", pairs)


def laid(parts, count):
    total, start = None, 0
    for part in parts:
        end = count - start - part.shape[0]
        wide = jnp.pad(part, ((start, end), (0, 0)))
        total = wide if total is None else total + wide
        start += part.shape[0]
    return total


def packed(value, scale, *rows):
    parts = [value * jnp.exp2(-scale), *rows]
    return laid(parts, value.shape[0] + 16).astype(jnp.float16)


def whole_decay(rows):
    return rows[0:1] + rows[1:2] / 256.0 + rows[2:3] / 65536.0


def carry_over(state_end, adjoint_end, info):
    count = lax.axis_size("tm")
    odd = info[5:6] > 0.5
    places = [info[6 + d : 7 + d] for d in range(count // 2)]
    half = state_end.shape[0] // 2

    def both(low, high, scale_low, scale_high, rows):
        parts = [low * jnp.exp2(-scale_low), high * jnp.exp2(-scale_high), rows]
        return laid(parts, 2 * half + 16).astype(jnp.float16)

    def give(value, mine):
        low, high = value[:half], value[half:]
        return jnp.where(odd, high, low) if mine else jnp.where(odd, low, high)

    got = swap(
        both(give(state_end, False), give(adjoint_end, False), info[0:1], info[1:2], info[:5]), 1, 0
    ).astype(F32)
    their_info = got[2 * half : 2 * half + 5]
    total, their_total = whole_decay(info[2:5]), whole_decay(their_info[2:5])
    even_total = jnp.where(odd, their_total, total)
    odd_total = jnp.where(odd, total, their_total)
    state_mine, adjoint_mine = give(state_end, True), give(adjoint_end, True)
    state_theirs = got[:half] * jnp.exp2(their_info[0:1])
    adjoint_theirs = got[half : 2 * half] * jnp.exp2(their_info[1:2])
    state_even = jnp.where(odd, state_theirs, state_mine)
    state_odd = jnp.where(odd, state_mine, state_theirs)
    adjoint_even = jnp.where(odd, adjoint_theirs, adjoint_mine)
    adjoint_odd = jnp.where(odd, adjoint_mine, adjoint_theirs)
    state_pair = odd_total * state_even + state_odd
    adjoint_pair = adjoint_even + even_total * adjoint_odd
    state_scale = jnp.maximum(info[0:1], their_info[0:1])
    adjoint_scale = jnp.maximum(info[1:2], their_info[1:2])

    messages = []
    bit = 1
    while bit < count // 2:
        later = places[bit] < places[0]
        scale = jnp.where(later, adjoint_scale, state_scale)
        value = jnp.where(later, adjoint_pair, state_pair)
        messages.append(packed(value, scale, scale, info[2:5], their_info[2:5]))
        bit *= 2
    received = {}
    for d in range(1, count // 2):
        received[d] = swap(messages[d.bit_length() - 1], 2 * d, 0).astype(F32)
    totals, values = {}, {}
    top_scale = jnp.maximum(state_scale, adjoint_scale)
    for d, got in received.items():
        rows = got[half : half + 7]
        totals[d] = whole_decay(rows[1:4]) * whole_decay(rows[4:7])
        values[d] = got[:half] * jnp.exp2(rows[0:1])
        top_scale = jnp.maximum(top_scale, rows[0:1])
    state_before = jnp.zeros_like(state_pair)
    adjoint_after = jnp.zeros_like(adjoint_pair)
    for d in received:
        through = jnp.ones_like(top_scale)
        for e in received:
            low = jnp.minimum(places[0], places[d])
            high = jnp.maximum(places[0], places[d])
            inside = (low < places[e]) & (places[e] < high)
            through = through * jnp.where(inside, totals[e], 1.0)
        term = through * values[d]
        state_before = state_before + jnp.where(places[d] < places[0], term, 0.0)
        adjoint_after = adjoint_after + jnp.where(places[d] > places[0], term, 0.0)

    state_inner = state_even + even_total * state_before
    adjoint_inner = adjoint_odd + odd_total * adjoint_after
    state_keep = jnp.where(odd, state_inner, state_before)
    state_send = jnp.where(odd, state_before, state_inner)
    adjoint_keep = jnp.where(odd, adjoint_after, adjoint_inner)
    adjoint_send = jnp.where(odd, adjoint_inner, adjoint_after)
    got = swap(both(state_send, adjoint_send, top_scale, top_scale, top_scale), 1, 0).astype(F32)
    scale = jnp.exp2(got[2 * half : 2 * half + 1])

    def joined(keep, other):
        return jnp.concatenate([jnp.where(odd, other, keep), jnp.where(odd, keep, other)], 0)

    return (
        joined(state_keep, got[:half] * scale),
        joined(adjoint_keep, got[half : 2 * half] * scale),
    )


def unpacked(got):
    rows = got.shape[-2] - 16
    wide = got.astype(F32)
    scale = wide[..., rows : rows + 1, :]
    return wide[..., :rows, :] * jnp.exp2(scale), scale


def shards(frames, cotangent, w_in, w_out, skip, log_decay):
    times, rows, cols, ch = frames.shape
    half = rows // 2
    place = jnp.stack([lax.axis_index("tile"), lax.axis_index("tm")]).astype(jnp.int32)
    place = lax.optimization_barrier(place)
    odd = place[0] % 2 == 1
    gain = skip[None, :]

    low = jnp.stack([frames[:, 0], cotangent[:, 0]])
    high = jnp.stack([frames[:, -1], cotangent[:, -1]])
    second = swap_across(jnp.where(odd, high, low))
    first = swap(jnp.where(odd, low, high), 0, 1)

    blocks = blocks_call(frames, cotangent, w_in, w_out, log_decay)
    states, adjoints, leaving, frame_taps, cot_taps, info = drive_call(
        place, frames, cotangent, first, second, blocks, log_decay
    )
    state_in, adjoint_in = carry_over(states[-1], leaving, info)
    states_bf, inflow_bf, first, second, in_part, out_part, info = grads_call(
        place, states, adjoints, state_in, adjoint_in, log_decay, frame_taps, cot_taps
    )

    out_scale, in_scale = info[0:1], info[1:2]
    odd, odd_tm, high_tile = (info[n : n + 1] > 0.5 for n in (2, 3, 4))
    scale = jnp.where(odd, in_scale, out_scale)
    message = packed(jnp.where(odd, in_part, out_part), scale, scale)
    message, first, second = lax.optimization_barrier((message, first, second))
    got, got_scale = unpacked(swap(message, 0, 1))
    value = jnp.where(odd, out_part, in_part) + got
    scale = jnp.maximum(jnp.where(odd, out_scale, in_scale), got_scale)
    second = swap_across(second)
    first = swap(first, 0, 1)

    bits = [((1, 0), odd_tm), ((0, 2), high_tile)] if lax.axis_size("tile") > 2 else [((1, 0), odd_tm)]
    parts = 2 ** len(bits)
    pieces = list(value.reshape(parts, -1, ch))
    for n, (_, high) in enumerate(bits):
        for d in range(parts):
            if not d >> n & 1:
                a, b = pieces[d], pieces[d + 2**n]
                pieces[d], pieces[d + 2**n] = jnp.where(high, b, a), jnp.where(high, a, b)

    def mask(d):
        chosen = [bit for n, (bit, _) in enumerate(bits) if d >> n & 1]
        return sum(b[0] for b in chosen), sum(b[1] for b in chosen)

    messages = [packed(pieces[d], scale, scale) for d in range(1, parts)]
    value = pieces[0]
    states_bf = states_bf.reshape(times, half, cols, 2 * ch)
    inflow_bf = inflow_bf.reshape(times, half, cols, 2 * ch)
    *messages, states_bf = lax.optimization_barrier((*messages, states_bf))
    received = [swap(m, *mask(d + 1)) for d, m in enumerate(messages)]
    output = output_call(place, states_bf, first, second, w_out, gain, frames, False)
    for got in received:
        got, got_scale = unpacked(got)
        value = value + got
        scale = jnp.maximum(scale, got_scale)

    left = []
    bit = 2
    while bit < lax.axis_size("tm"):
        left.append((bit, 0))
        bit *= 2
    bit = 4
    while bit < lax.axis_size("tile"):
        left.append((0, bit))
        bit *= 2
    waiting = inflow_bf
    for n in range(0, len(left), 2):
        group = left[n : n + 2]
        message = packed(value, scale, scale)
        message, output, waiting = lax.optimization_barrier((message, output, waiting))
        terms = [message]
        for d in range(1, 2 ** len(group)):
            chosen = [b for k, b in enumerate(group) if d >> k & 1]
            terms.append(swap(message, sum(b[0] for b in chosen), sum(b[1] for b in chosen)))
        terms = [unpacked(term) for term in terms]
        while len(terms) > 1:
            terms = [
                (a[0] + b[0], jnp.maximum(a[1], b[1])) for a, b in zip(terms[::2], terms[1::2])
            ]
        value, scale = terms[0]
    grad_frames = output_call(place, waiting, first, second, w_in, gain, cotangent, True)

    message = packed(value, scale, scale)
    message, grad_frames = lax.optimization_barrier((message, grad_frames))
    gathered = [message] + [swap(message, *mask(d)) for d in range(1, parts)]
    for _, high in bits:
        gathered = [
            (jnp.where(high, b, a), jnp.where(high, a, b))
            for a, b in zip(gathered[::2], gathered[1::2])
        ]
        gathered = [jnp.concatenate(pair, 0) for pair in gathered]
    (mine,) = gathered
    mine = lax.optimization_barrier(mine)
    theirs = swap(mine, 0, 1)
    factor = 1.0 / math.sqrt(
        times * lax.axis_size("tm") * rows * lax.axis_size("tile") * cols
    )
    results = []
    for chosen in (jnp.where(odd, theirs, mine), jnp.where(odd, mine, theirs)):
        whole, _ = unpacked(chosen.reshape(parts, -1, ch))
        results.append((whole * factor).reshape(3, 3, ch, ch))
    return (output, grad_frames, results[0], results[1])


def solution(mesh):
    placed = (
        P("tm", "tile", None, None),
        P("tm", "tile", None, None),
        P(),
        P(),
        P(),
        P("tm", None),
    )
    return jax.shard_map(
        shards,
        mesh=mesh,
        in_specs=placed,
        out_specs=(P("tm", "tile", None, None), P("tm", "tile", None, None), P(), P()),
        check_vma=False,
    )
```

```python
import functools
import math

import jax
import jax.numpy as jnp
from jax import lax
from jax.experimental import pallas as pl
from jax.experimental.pallas import tpu as pltpu
from jax.sharding import PartitionSpec as P

F32 = jnp.float32
BF16 = jnp.bfloat16
VMEM_LIMIT = 24 * 1024 * 1024


def fill_pairs(pairs, field, top, bottom):
    half = field.shape[1] // 2
    ch = field.shape[3]
    pairs[:, 0, :, :ch] = top[:, 0]
    pairs[:, half, :, ch:] = bottom[:, 0]
    for i in range(half):
        pairs[:, i, :, ch:] = field[:, 2 * i]
        pairs[:, i + 1, :, :ch] = field[:, 2 * i + 1]


def fill_pairs_from_pairs(pairs, field, top, bottom):
    half = field.shape[1]
    ch = field.shape[3] // 2
    pairs[:, 0, :, :ch] = top[:, 0]
    pairs[:, half, :, ch:] = bottom[:, 0]
    pairs[:, :half, :, ch:] = field[:, :, :, :ch]
    pairs[:, 1:, :, :ch] = field[:, :, :, ch:]


def column_taps(flat, cols):
    wide = flat.astype(F32)
    count = wide.shape[0]
    col = lax.broadcasted_iota(jnp.int32, wide.shape, 0) % cols
    left = jnp.where(col == 0, 0.0, pltpu.roll(wide, 1, 0)).astype(flat.dtype)
    right = jnp.where(col == cols - 1, 0.0, pltpu.roll(wide, count - 1, 0)).astype(flat.dtype)
    return left, flat, right


def fill_weights(blocks, weight, flip):
    ch = weight.shape[2]
    zero = jnp.zeros((ch, ch), weight.dtype)
    for j in range(3):
        for b in range(2):
            for k in range(2):
                for n in range(2):
                    tap = 2 * b + k - n
                    ok = 0 <= tap <= 2
                    if flip:
                        value = weight[2 - tap, 2 - j] if ok else zero
                        blocks[j, b, n * ch : (n + 1) * ch, k * ch : (k + 1) * ch] = value
                    else:
                        value = weight[tap, j] if ok else zero
                        blocks[j, b, k * ch : (k + 1) * ch, n * ch : (n + 1) * ch] = value


def conv_pairs(taps, blocks, rows_out, cols, flip):
    dims = (((1,), (1,)), ((), ())) if flip else (((1,), (0,)), ((), ()))
    total = None
    for j in range(3):
        for b in range(2):
            part = lax.dot_general(
                taps[j][b * cols : b * cols + rows_out],
                blocks[j, b],
                dims,
                preferred_element_type=F32,
            )
            total = part if total is None else total + part
    return total


def pick_halos(first, second, index, odd, times):
    one = first[index].astype(F32)
    two = second[index].astype(F32)
    upper = jnp.where(odd, one, two).astype(BF16)
    lower = jnp.where(odd, two, one).astype(BF16)
    return upper[:, None], lower[:, None]


def exponent(value):
    top = jnp.max(jnp.abs(value), axis=0, keepdims=True)
    return jnp.ceil(jnp.log2(jnp.maximum(top, 1e-30)))


def decays(log_decay):
    wide = jnp.concatenate([log_decay, log_decay], 1)
    times = wide.shape[0]
    sums = [wide[0:1]]
    for t in range(1, times):
        sums.append(sums[-1] + wide[t : t + 1])
    rate = [jnp.exp(wide[t : t + 1]) for t in range(times)]
    reach = [jnp.exp(total) for total in sums]
    tail = [jnp.exp(sums[-1] - total) for total in sums]
    return rate, reach, tail


def blocks_kernel(frames, cotangent, w_in, w_out, log_decay, blocks):
    fill_weights(blocks.at[0], w_in, False)
    fill_weights(blocks.at[1], w_out, True)


def blocks_call(frames, cotangent, w_in, w_out, log_decay):
    ch = w_in.shape[2]
    return pl.pallas_call(
        blocks_kernel,
        out_shape=jax.ShapeDtypeStruct((2, 3, 2, 2 * ch, 2 * ch), BF16),
        compiler_params=pltpu.CompilerParams(vmem_limit_bytes=VMEM_LIMIT),
        cost_estimate=pl.CostEstimate(flops=0, bytes_accessed=10 << 20, transcendentals=0),
        name="blocks",
    )(frames, cotangent, w_in, w_out, log_decay)


def drive_kernel(
    place,
    frames,
    cotangent,
    first,
    second,
    blocks,
    log_decay,
    states,
    adjoints,
    leaving,
    frame_taps,
    cot_taps,
    info,
    pairs,
):
    times, rows, cols, ch = frames.shape
    half = rows // 2
    odd = lax.rem(place[0], 2) == 1
    rate, reach, _ = decays(log_decay[...])
    fields = ((frames, states, frame_taps), (cotangent, adjoints, cot_taps))
    for index, (field, result, taps_out) in enumerate(fields):
        flip = index == 1
        top, bottom = pick_halos(first, second, index, odd, times)
        fill_pairs(pairs.at[index], field, top, bottom)
        carry = None
        for step in range(times):
            t = times - 1 - step if flip else step
            taps = column_taps(pairs[index, t].reshape((half + 1) * cols, 2 * ch), cols)
            for j in range(3):
                taps_out[j, t] = taps[j]
            value = conv_pairs(taps, blocks.at[index], half * cols, cols, flip)
            if flip:
                value = value if carry is None else value + carry
                carry = rate[t] * value
            else:
                value = (1.0 - rate[t]) * value
                value = value if carry is None else rate[t] * carry + value
                carry = value
            result[t] = value
        if flip:
            leaving[...] = carry
        info[index : index + 1, :] = exponent(carry)
    total = reach[-1]
    high = total.astype(BF16).astype(F32)
    rest = (total - high) * 256.0
    middle = rest.astype(BF16).astype(F32)
    low = ((rest - middle) * 256.0).astype(BF16).astype(F32)
    info[2:3, :] = high
    info[3:4, :] = middle
    info[4:5, :] = low
    row = jnp.zeros((1, 2 * ch), F32)
    info[5:6, :] = row + lax.rem(place[1], 2).astype(F32)
    info[6:7, :] = row + lax.rem(lax.div(place[1], 2), 2).astype(F32)
    for d in range(info.shape[0] - 7):
        info[7 + d : 8 + d, :] = row + (lax.div(place[1], 4) ^ d).astype(F32)


def drive_call(place, frames, cotangent, first, second, blocks, log_decay):
    times, rows, cols, ch = frames.shape
    half = rows // 2
    field = jax.ShapeDtypeStruct((times, half * cols, 2 * ch), F32)
    rows_info = (7 + lax.axis_size("tm") // 4 + 15) // 16 * 16
    taps = jax.ShapeDtypeStruct((3, times, (half + 1) * cols, 2 * ch), BF16)
    return pl.pallas_call(
        drive_kernel,
        in_specs=[pl.BlockSpec(memory_space=pltpu.SMEM)]
        + [pl.BlockSpec(memory_space=pltpu.VMEM)] * 6,
        out_shape=(
            field,
            field,
            jax.ShapeDtypeStruct(field.shape[1:], F32),
            taps,
            taps,
            jax.ShapeDtypeStruct((rows_info, 2 * ch), F32),
        ),
        scratch_shapes=[
            pltpu.VMEM((2, times, half + 1, cols, 2 * ch), BF16),
        ],
        compiler_params=pltpu.CompilerParams(vmem_limit_bytes=VMEM_LIMIT),
        cost_estimate=pl.CostEstimate(
            flops=times * rows * cols * ch * ch * 48, bytes_accessed=12 << 20, transcendentals=0
        ),
        name="drive",
    )(place, frames, cotangent, first, second, blocks, log_decay)


def grads_kernel(
    place,
    states,
    adjoints,
    state_in,
    adjoint_in,
    log_decay,
    frame_taps,
    cot_taps,
    states_bf,
    inflow_bf,
    first,
    second,
    grads_in,
    grads_out,
    info,
    turned,
):
    times, count, width = states.shape
    ch = width // 2
    cols = frame_taps.shape[2] - count
    odd = lax.rem(place[0], 2) == 1
    rate, reach, tail = decays(log_decay[...])
    add = state_in[...]
    back = adjoint_in[...]
    for t in range(times):
        value = (states[t] + reach[t] * add).astype(BF16)
        states_bf[t] = value
        turned[0, t] = value.T
        value = ((1.0 - rate[t]) * (adjoints[t] + tail[t] * back)).astype(BF16)
        inflow_bf[t] = value
        turned[1, t] = value.T
        for index, field in enumerate((states_bf, inflow_bf)):
            low = field[t, :cols, :ch].astype(F32)
            high = field[t, count - cols :, ch:].astype(F32)
            first[index, t] = jnp.where(odd, low, high).astype(BF16)
            second[index, t] = jnp.where(odd, high, low).astype(BF16)
    for index, (taps, grads) in enumerate(((cot_taps, grads_out), (frame_taps, grads_in))):
        largest = None
        for j in range(3):
            blocks = []
            for b in range(2):
                total = None
                for t in range(times):
                    part = jnp.dot(
                        turned[index, t],
                        taps[j, t, b * cols : b * cols + count],
                        preferred_element_type=F32,
                    )
                    total = part if total is None else total + part
                blocks.append(total)
            for tap in range(3):
                total = None
                for b in range(2):
                    for c in range(2):
                        a = 2 * b + c - tap
                        if a in (0, 1):
                            part = blocks[b][a * ch : (a + 1) * ch, c * ch : (c + 1) * ch]
                            total = part if total is None else total + part
                if index == 0:
                    spot = (2 - tap) * 3 + 2 - j
                else:
                    spot = tap * 3 + j
                    total = total.T
                grads[spot * ch : (spot + 1) * ch, :] = total
                top = jnp.max(jnp.abs(total), axis=0, keepdims=True)
                largest = top if largest is None else jnp.maximum(largest, top)
        info[index : index + 1, :] = exponent(largest)
    row = jnp.zeros((1, ch), F32)
    info[2:3, :] = row + lax.rem(place[0], 2).astype(F32)
    info[3:4, :] = row + lax.rem(place[1], 2).astype(F32)
    info[4:5, :] = row + lax.rem(lax.div(place[0], 2), 2).astype(F32)
    info[5:, :] = jnp.zeros((info.shape[0] - 5, ch), F32)


def grads_call(place, states, adjoints, state_in, adjoint_in, log_decay, frame_taps, cot_taps):
    times, count, width = states.shape
    ch = width // 2
    cols = frame_taps.shape[2] - count
    field = jax.ShapeDtypeStruct((times, count, width), BF16)
    edge = jax.ShapeDtypeStruct((2, times, cols, ch), BF16)
    grads = jax.ShapeDtypeStruct((9 * ch, ch), F32)
    return pl.pallas_call(
        grads_kernel,
        in_specs=[pl.BlockSpec(memory_space=pltpu.SMEM)]
        + [pl.BlockSpec(memory_space=pltpu.VMEM)] * 7,
        out_shape=(field, field, edge, edge, grads, grads, jax.ShapeDtypeStruct((16, ch), F32)),
        scratch_shapes=[pltpu.VMEM((2, times, width, count), BF16)],
        compiler_params=pltpu.CompilerParams(vmem_limit_bytes=VMEM_LIMIT),
        cost_estimate=pl.CostEstimate(
            flops=times * count * ch * ch * 96, bytes_accessed=12 << 20, transcendentals=0
        ),
        name="grads",
    )(place, states, adjoints, state_in, adjoint_in, log_decay, frame_taps, cot_taps)


def output_kernel(place, field, first, second, weight, skip, direct, out, pairs, blocks, *, flip):
    times, half, cols, width = field.shape
    ch = width // 2
    fill_weights(blocks, weight, flip)
    top, bottom = pick_halos(first, second, int(flip), lax.rem(place[0], 2) == 1, times)
    fill_pairs_from_pairs(pairs, field, top, bottom)
    gain = skip[...]
    for t in range(times):
        taps = column_taps(pairs[t].reshape((half + 1) * cols, width), cols)
        value = conv_pairs(taps, blocks, half * cols, cols, flip).reshape(half, cols, width)
        for i in range(half):
            for c in range(2):
                base = gain * direct[t, 2 * i + c].astype(F32)
                out[t, 2 * i + c] = (value[i, :, c * ch : (c + 1) * ch] + base).astype(BF16)


def output_call(place, field, first, second, weight, skip, direct, flip):
    times, half, cols, width = field.shape
    ch = width // 2
    return pl.pallas_call(
        functools.partial(output_kernel, flip=flip),
        in_specs=[pl.BlockSpec(memory_space=pltpu.SMEM)]
        + [pl.BlockSpec(memory_space=pltpu.VMEM)] * 6,
        out_shape=jax.ShapeDtypeStruct(direct.shape, BF16),
        scratch_shapes=[
            pltpu.VMEM((times, half + 1, cols, width), BF16),
            pltpu.VMEM((3, 2, width, width), BF16),
        ],
        compiler_params=pltpu.CompilerParams(vmem_limit_bytes=VMEM_LIMIT),
        cost_estimate=pl.CostEstimate(
            flops=times * half * cols * ch * ch * 48, bytes_accessed=4 << 20, transcendentals=0
        ),
        name="grad_frames" if flip else "output",
    )(place, field, first, second, weight, skip, direct)


def swap(value, tm_bits, tile_bits):
    tiles = lax.axis_size("tile")
    mask = tm_bits * tiles + tile_bits
    count = lax.axis_size("tm") * tiles
    return lax.ppermute(value, ("tm", "tile"), [(i, i ^ mask) for i in range(count)])


def swap_across(value):
    count = lax.axis_size("tile")
    pairs = []
    for i in range(1, count - 1, 2):
        pairs += [(i, i + 1), (i + 1, i)]
    return lax.ppermute(value, "tile", pairs)


def laid(parts, count):
    total, start = None, 0
    for part in parts:
        end = count - start - part.shape[0]
        wide = jnp.pad(part, ((start, end), (0, 0)))
        total = wide if total is None else total + wide
        start += part.shape[0]
    return total


def packed(value, scale, *rows):
    parts = [value * jnp.exp2(-scale), *rows]
    return laid(parts, value.shape[0] + 16).astype(jnp.float16)


def whole_decay(rows):
    return rows[0:1] + rows[1:2] / 256.0 + rows[2:3] / 65536.0


def by_place(values, flags):
    values = list(values)
    for n, flag in enumerate(flags):
        for d in range(len(values)):
            if not d >> n & 1:
                a, b = values[d], values[d + 2**n]
                values[d], values[d + 2**n] = jnp.where(flag, b, a), jnp.where(flag, a, b)
    return values


def carry_over(state_end, adjoint_end, info):
    squares = lax.axis_size("tm") // 4
    flags = [info[5:6] > 0.5, info[6:7] > 0.5]
    places = [info[7 + d : 8 + d] for d in range(squares)]
    part = state_end.shape[0] // 4
    width = state_end.shape[1]

    def both(low, high, scale_low, scale_high, rows):
        parts = [low * jnp.exp2(-scale_low), high * jnp.exp2(-scale_high), rows]
        return laid(parts, 2 * part + 16).astype(jnp.float16)

    def quarters(value):
        return by_place([value[n * part : (n + 1) * part] for n in range(4)], flags)

    states, adjoints = quarters(state_end), quarters(adjoint_end)
    messages = [both(states[d], adjoints[d], info[0:1], info[1:2], info[:5]) for d in (1, 2, 3)]
    received = [swap(m, d + 1, 0).astype(F32) for d, m in enumerate(messages)]
    rows = [info[:5]] + [got[2 * part : 2 * part + 5] for got in received]
    state_scale = functools.reduce(jnp.maximum, [row[0:1] for row in rows])
    adjoint_scale = functools.reduce(jnp.maximum, [row[1:2] for row in rows])
    states = [states[0]] + [
        got[:part] * jnp.exp2(row[0:1]) for got, row in zip(received, rows[1:])
    ]
    adjoints = [adjoints[0]] + [
        got[part : 2 * part] * jnp.exp2(row[1:2]) for got, row in zip(received, rows[1:])
    ]
    states, adjoints = by_place(states, flags), by_place(adjoints, flags)
    decay_rows = by_place([row[2:5] for row in rows], flags)
    totals = [whole_decay(row) for row in decay_rows]

    one = jnp.ones((1, width), F32)
    zero = jnp.zeros((part, width), F32)
    before, reach = [zero], [one]
    for n in range(4):
        before.append(totals[n] * before[-1] + states[n])
        reach.append(reach[-1] * totals[n])
    after, back = [zero], [one]
    for n in (3, 2, 1, 0):
        after.insert(0, adjoints[n] + totals[n] * after[0])
        back.insert(0, back[0] * totals[n])
    state_square, adjoint_square = before.pop(), after.pop(0)
    back.pop(0)

    messages = []
    bit = 1
    while bit < squares:
        later = places[bit] < places[0]
        scale = jnp.where(later, adjoint_scale, state_scale)
        value = jnp.where(later, adjoint_square, state_square)
        messages.append(packed(value, scale, scale, *decay_rows))
        bit *= 2
    through_square, values = {}, {}
    top_scale = jnp.maximum(state_scale, adjoint_scale)
    for d in range(1, squares):
        got = swap(messages[d.bit_length() - 1], 4 * d, 0).astype(F32)
        there = [got[part + 1 + 3 * n : part + 4 + 3 * n] for n in range(4)]
        through_square[d] = functools.reduce(jnp.multiply, [whole_decay(row) for row in there])
        values[d] = got[:part] * jnp.exp2(got[part : part + 1])
        top_scale = jnp.maximum(top_scale, got[part : part + 1])
    state_before, adjoint_after = zero, zero
    for d in values:
        term = values[d]
        if squares > 2:
            through = one
            for e in values:
                low = jnp.minimum(places[0], places[d])
                high = jnp.maximum(places[0], places[d])
                inside = (low < places[e]) & (places[e] < high)
                through = through * jnp.where(inside, through_square[e], 1.0)
            term = through * term
        state_before = state_before + jnp.where(places[d] < places[0], term, 0.0)
        adjoint_after = adjoint_after + jnp.where(places[d] > places[0], term, 0.0)

    states = by_place([before[n] + reach[n] * state_before for n in range(4)], flags)
    adjoints = by_place([after[n] + back[n] * adjoint_after for n in range(4)], flags)
    messages = [both(states[d], adjoints[d], top_scale, top_scale, top_scale) for d in (1, 2, 3)]
    received = [swap(m, d + 1, 0).astype(F32) for d, m in enumerate(messages)]
    scales = [jnp.exp2(got[2 * part : 2 * part + 1]) for got in received]
    states = [states[0]] + [got[:part] * s for got, s in zip(received, scales)]
    adjoints = [adjoints[0]] + [got[part : 2 * part] * s for got, s in zip(received, scales)]
    return (
        jnp.concatenate(by_place(states, flags), 0),
        jnp.concatenate(by_place(adjoints, flags), 0),
    )


def unpacked(got):
    rows = got.shape[-2] - 16
    wide = got.astype(F32)
    scale = wide[..., rows : rows + 1, :]
    return wide[..., :rows, :] * jnp.exp2(scale), scale


def shards(frames, cotangent, w_in, w_out, skip, log_decay):
    times, rows, cols, ch = frames.shape
    half = rows // 2
    place = jnp.stack([lax.axis_index("tile"), lax.axis_index("tm")]).astype(jnp.int32)
    place = lax.optimization_barrier(place)
    odd = place[0] % 2 == 1
    gain = skip[None, :]

    low = jnp.stack([frames[:, 0], cotangent[:, 0]])
    high = jnp.stack([frames[:, -1], cotangent[:, -1]])
    second = swap_across(jnp.where(odd, high, low))
    first = swap(jnp.where(odd, low, high), 0, 1)

    blocks = blocks_call(frames, cotangent, w_in, w_out, log_decay)
    states, adjoints, leaving, frame_taps, cot_taps, info = drive_call(
        place, frames, cotangent, first, second, blocks, log_decay
    )
    state_in, adjoint_in = carry_over(states[-1], leaving, info)
    states_bf, inflow_bf, first, second, in_part, out_part, info = grads_call(
        place, states, adjoints, state_in, adjoint_in, log_decay, frame_taps, cot_taps
    )

    out_scale, in_scale = info[0:1], info[1:2]
    odd, odd_tm, high_tile = (info[n : n + 1] > 0.5 for n in (2, 3, 4))
    scale = jnp.where(odd, in_scale, out_scale)
    message = packed(jnp.where(odd, in_part, out_part), scale, scale)
    message, first, second = lax.optimization_barrier((message, first, second))
    got, got_scale = unpacked(swap(message, 0, 1))
    value = jnp.where(odd, out_part, in_part) + got
    scale = jnp.maximum(jnp.where(odd, out_scale, in_scale), got_scale)
    second = swap_across(second)
    first = swap(first, 0, 1)

    bits = [((1, 0), odd_tm), ((0, 2), high_tile)] if lax.axis_size("tile") > 2 else [((1, 0), odd_tm)]
    parts = 2 ** len(bits)
    pieces = list(value.reshape(parts, -1, ch))
    for n, (_, high) in enumerate(bits):
        for d in range(parts):
            if not d >> n & 1:
                a, b = pieces[d], pieces[d + 2**n]
                pieces[d], pieces[d + 2**n] = jnp.where(high, b, a), jnp.where(high, a, b)

    def mask(d):
        chosen = [bit for n, (bit, _) in enumerate(bits) if d >> n & 1]
        return sum(b[0] for b in chosen), sum(b[1] for b in chosen)

    messages = [packed(pieces[d], scale, scale) for d in range(1, parts)]
    value = pieces[0]
    states_bf = states_bf.reshape(times, half, cols, 2 * ch)
    inflow_bf = inflow_bf.reshape(times, half, cols, 2 * ch)
    *messages, states_bf = lax.optimization_barrier((*messages, states_bf))
    received = [swap(m, *mask(d + 1)) for d, m in enumerate(messages)]
    output = output_call(place, states_bf, first, second, w_out, gain, frames, False)
    for got in received:
        got, got_scale = unpacked(got)
        value = value + got
        scale = jnp.maximum(scale, got_scale)

    left = []
    bit = 2
    while bit < lax.axis_size("tm"):
        left.append((bit, 0))
        bit *= 2
    bit = 4
    while bit < lax.axis_size("tile"):
        left.append((0, bit))
        bit *= 2
    waiting = inflow_bf
    for n in range(0, len(left), 2):
        group = left[n : n + 2]
        message = packed(value, scale, scale)
        message, output, waiting = lax.optimization_barrier((message, output, waiting))
        terms = [message]
        for d in range(1, 2 ** len(group)):
            chosen = [b for k, b in enumerate(group) if d >> k & 1]
            terms.append(swap(message, sum(b[0] for b in chosen), sum(b[1] for b in chosen)))
        terms = [unpacked(term) for term in terms]
        while len(terms) > 1:
            terms = [
                (a[0] + b[0], jnp.maximum(a[1], b[1])) for a, b in zip(terms[::2], terms[1::2])
            ]
        value, scale = terms[0]
    grad_frames = output_call(place, waiting, first, second, w_in, gain, cotangent, True)

    message = packed(value, scale, scale)
    message, grad_frames = lax.optimization_barrier((message, grad_frames))
    gathered = [message] + [swap(message, *mask(d)) for d in range(1, parts)]
    for _, high in bits:
        gathered = [
            (jnp.where(high, b, a), jnp.where(high, a, b))
            for a, b in zip(gathered[::2], gathered[1::2])
        ]
        gathered = [jnp.concatenate(pair, 0) for pair in gathered]
    (mine,) = gathered
    mine = lax.optimization_barrier(mine)
    theirs = swap(mine, 0, 1)
    factor = 1.0 / math.sqrt(
        times * lax.axis_size("tm") * rows * lax.axis_size("tile") * cols
    )
    results = []
    for chosen in (jnp.where(odd, theirs, mine), jnp.where(odd, mine, theirs)):
        whole, _ = unpacked(chosen.reshape(parts, -1, ch))
        results.append((whole * factor).reshape(3, 3, ch, ch))
    return (output, grad_frames, results[0], results[1])


def solution(mesh):
    placed = (
        P("tm", "tile", None, None),
        P("tm", "tile", None, None),
        P(),
        P(),
        P(),
        P("tm", None),
    )
    return jax.shard_map(
        shards,
        mesh=mesh,
        in_specs=placed,
        out_specs=(P("tm", "tile", None, None), P("tm", "tile", None, None), P(), P()),
        check_vma=False,
    )
```

```python
import functools
import math

import jax
import jax.numpy as jnp
from jax import lax
from jax.experimental import pallas as pl
from jax.experimental.pallas import tpu as pltpu
from jax.sharding import PartitionSpec as P

F32 = jnp.float32
BF16 = jnp.bfloat16
VMEM_LIMIT = 24 * 1024 * 1024


def fill_pairs(pairs, field, top, bottom):
    half = field.shape[1] // 2
    ch = field.shape[3]
    pairs[:, 0, :, :ch] = top[:, 0]
    pairs[:, half, :, ch:] = bottom[:, 0]
    for i in range(half):
        pairs[:, i, :, ch:] = field[:, 2 * i]
        pairs[:, i + 1, :, :ch] = field[:, 2 * i + 1]


def fill_pairs_from_pairs(pairs, field, top, bottom):
    half = field.shape[1]
    ch = field.shape[3] // 2
    pairs[:, 0, :, :ch] = top[:, 0]
    pairs[:, half, :, ch:] = bottom[:, 0]
    pairs[:, :half, :, ch:] = field[:, :, :, :ch]
    pairs[:, 1:, :, :ch] = field[:, :, :, ch:]


def column_taps(flat, cols):
    wide = flat.astype(F32)
    count = wide.shape[0]
    col = lax.broadcasted_iota(jnp.int32, wide.shape, 0) % cols
    left = jnp.where(col == 0, 0.0, pltpu.roll(wide, 1, 0)).astype(flat.dtype)
    right = jnp.where(col == cols - 1, 0.0, pltpu.roll(wide, count - 1, 0)).astype(flat.dtype)
    return left, flat, right


def fill_weights(blocks, weight, flip):
    ch = weight.shape[2]
    zero = jnp.zeros((ch, ch), weight.dtype)
    for j in range(3):
        for b in range(2):
            for k in range(2):
                for n in range(2):
                    tap = 2 * b + k - n
                    ok = 0 <= tap <= 2
                    if flip:
                        value = weight[2 - tap, 2 - j] if ok else zero
                        blocks[j, b, n * ch : (n + 1) * ch, k * ch : (k + 1) * ch] = value
                    else:
                        value = weight[tap, j] if ok else zero
                        blocks[j, b, k * ch : (k + 1) * ch, n * ch : (n + 1) * ch] = value


def conv_pairs(taps, blocks, rows_out, cols, flip):
    dims = (((1,), (1,)), ((), ())) if flip else (((1,), (0,)), ((), ()))
    total = None
    for j in range(3):
        for b in range(2):
            part = lax.dot_general(
                taps[j][b * cols : b * cols + rows_out],
                blocks[j, b],
                dims,
                preferred_element_type=F32,
            )
            total = part if total is None else total + part
    return total


def pick_halos(first, second, index, odd, times):
    one = first[index].astype(F32)
    two = second[index].astype(F32)
    upper = jnp.where(odd, one, two).astype(BF16)
    lower = jnp.where(odd, two, one).astype(BF16)
    return upper[:, None], lower[:, None]


def exponent(value):
    top = jnp.max(jnp.abs(value), axis=0, keepdims=True)
    return jnp.ceil(jnp.log2(jnp.maximum(top, 1e-30)))


def decays(log_decay):
    wide = jnp.concatenate([log_decay, log_decay], 1)
    times = wide.shape[0]
    sums = [wide[0:1]]
    for t in range(1, times):
        sums.append(sums[-1] + wide[t : t + 1])
    rate = [jnp.exp(wide[t : t + 1]) for t in range(times)]
    reach = [jnp.exp(total) for total in sums]
    tail = [jnp.exp(sums[-1] - total) for total in sums]
    return rate, reach, tail


def blocks_kernel(fields, weights, log_decay, blocks):
    fill_weights(blocks.at[0], weights.at[0], False)
    fill_weights(blocks.at[1], weights.at[1], True)


def blocks_call(fields, weights, log_decay):
    ch = weights.shape[3]
    return pl.pallas_call(
        blocks_kernel,
        out_shape=jax.ShapeDtypeStruct((2, 3, 2, 2 * ch, 2 * ch), BF16),
        compiler_params=pltpu.CompilerParams(vmem_limit_bytes=VMEM_LIMIT),
        cost_estimate=pl.CostEstimate(flops=0, bytes_accessed=10 << 20, transcendentals=0),
        name="blocks",
    )(fields, weights, log_decay)


def drive_kernel(
    place,
    fields,
    first,
    second,
    blocks,
    log_decay,
    states,
    adjoints,
    leaving,
    frame_taps,
    cot_taps,
    info,
    pairs,
):
    _, times, rows, cols, ch = fields.shape
    half = rows // 2
    odd = lax.rem(place[0], 2) == 1
    rate, reach, _ = decays(log_decay[...])
    results = ((states, frame_taps), (adjoints, cot_taps))
    for index, (result, taps_out) in enumerate(results):
        flip = index == 1
        top, bottom = pick_halos(first, second, index, odd, times)
        fill_pairs(pairs.at[index], fields.at[index], top, bottom)
        carry = None
        for step in range(times):
            t = times - 1 - step if flip else step
            taps = column_taps(pairs[index, t].reshape((half + 1) * cols, 2 * ch), cols)
            for j in range(3):
                taps_out[j, t] = taps[j]
            value = conv_pairs(taps, blocks.at[index], half * cols, cols, flip)
            if flip:
                value = value if carry is None else value + carry
                carry = rate[t] * value
            else:
                value = (1.0 - rate[t]) * value
                value = value if carry is None else rate[t] * carry + value
                carry = value
            result[t] = value
        if flip:
            leaving[...] = carry
        info[index : index + 1, :] = exponent(carry)
    total = reach[-1]
    high = total.astype(BF16).astype(F32)
    rest = (total - high) * 256.0
    middle = rest.astype(BF16).astype(F32)
    low = ((rest - middle) * 256.0).astype(BF16).astype(F32)
    info[2:3, :] = high
    info[3:4, :] = middle
    info[4:5, :] = low
    row = jnp.zeros((1, 2 * ch), F32)
    info[5:6, :] = row + lax.rem(place[1], 2).astype(F32)
    info[6:7, :] = row + lax.rem(lax.div(place[1], 2), 2).astype(F32)
    for d in range(info.shape[0] - 7):
        info[7 + d : 8 + d, :] = row + (lax.div(place[1], 4) ^ d).astype(F32)


def drive_call(place, fields, first, second, blocks, log_decay):
    _, times, rows, cols, ch = fields.shape
    half = rows // 2
    field = jax.ShapeDtypeStruct((times, half * cols, 2 * ch), F32)
    rows_info = (7 + lax.axis_size("tm") // 4 + 15) // 16 * 16
    taps = jax.ShapeDtypeStruct((3, times, (half + 1) * cols, 2 * ch), BF16)
    return pl.pallas_call(
        drive_kernel,
        in_specs=[pl.BlockSpec(memory_space=pltpu.SMEM)]
        + [pl.BlockSpec(memory_space=pltpu.VMEM)] * 5,
        out_shape=(
            field,
            field,
            jax.ShapeDtypeStruct(field.shape[1:], F32),
            taps,
            taps,
            jax.ShapeDtypeStruct((rows_info, 2 * ch), F32),
        ),
        scratch_shapes=[
            pltpu.VMEM((2, times, half + 1, cols, 2 * ch), BF16),
        ],
        compiler_params=pltpu.CompilerParams(vmem_limit_bytes=VMEM_LIMIT),
        cost_estimate=pl.CostEstimate(
            flops=times * rows * cols * ch * ch * 48, bytes_accessed=12 << 20, transcendentals=0
        ),
        name="drive",
    )(place, fields, first, second, blocks, log_decay)


def grads_kernel(
    place,
    states,
    adjoints,
    state_in,
    adjoint_in,
    log_decay,
    frame_taps,
    cot_taps,
    states_bf,
    inflow_bf,
    first,
    second,
    grads_in,
    grads_out,
    info,
    turned,
):
    times, count, width = states.shape
    ch = width // 2
    cols = frame_taps.shape[2] - count
    odd = lax.rem(place[0], 2) == 1
    rate, reach, tail = decays(log_decay[...])
    add = state_in[...]
    back = adjoint_in[...]
    for t in range(times):
        value = (states[t] + reach[t] * add).astype(BF16)
        states_bf[t] = value
        turned[0, t] = value.T
        value = ((1.0 - rate[t]) * (adjoints[t] + tail[t] * back)).astype(BF16)
        inflow_bf[t] = value
        turned[1, t] = value.T
        for index, field in enumerate((states_bf, inflow_bf)):
            low = field[t, :cols, :ch].astype(F32)
            high = field[t, count - cols :, ch:].astype(F32)
            first[index, t] = jnp.where(odd, low, high).astype(BF16)
            second[index, t] = jnp.where(odd, high, low).astype(BF16)
    for index, (taps, grads) in enumerate(((cot_taps, grads_out), (frame_taps, grads_in))):
        largest = None
        for j in range(3):
            blocks = []
            for b in range(2):
                total = None
                for t in range(times):
                    part = jnp.dot(
                        turned[index, t],
                        taps[j, t, b * cols : b * cols + count],
                        preferred_element_type=F32,
                    )
                    total = part if total is None else total + part
                blocks.append(total)
            for tap in range(3):
                total = None
                for b in range(2):
                    for c in range(2):
                        a = 2 * b + c - tap
                        if a in (0, 1):
                            part = blocks[b][a * ch : (a + 1) * ch, c * ch : (c + 1) * ch]
                            total = part if total is None else total + part
                if index == 0:
                    spot = (2 - tap) * 3 + 2 - j
                else:
                    spot = tap * 3 + j
                    total = total.T
                grads[spot * ch : (spot + 1) * ch, :] = total
                top = jnp.max(jnp.abs(total), axis=0, keepdims=True)
                largest = top if largest is None else jnp.maximum(largest, top)
        info[index : index + 1, :] = exponent(largest)
    row = jnp.zeros((1, ch), F32)
    info[2:3, :] = row + lax.rem(place[0], 2).astype(F32)
    info[3:4, :] = row + lax.rem(place[1], 2).astype(F32)
    info[4:5, :] = row + lax.rem(lax.div(place[0], 2), 2).astype(F32)
    info[5:, :] = jnp.zeros((info.shape[0] - 5, ch), F32)


def grads_call(place, states, adjoints, state_in, adjoint_in, log_decay, frame_taps, cot_taps):
    times, count, width = states.shape
    ch = width // 2
    cols = frame_taps.shape[2] - count
    field = jax.ShapeDtypeStruct((times, count, width), BF16)
    edge = jax.ShapeDtypeStruct((2, times, cols, ch), BF16)
    grads = jax.ShapeDtypeStruct((9 * ch, ch), F32)
    return pl.pallas_call(
        grads_kernel,
        in_specs=[pl.BlockSpec(memory_space=pltpu.SMEM)]
        + [pl.BlockSpec(memory_space=pltpu.VMEM)] * 7,
        out_shape=(field, field, edge, edge, grads, grads, jax.ShapeDtypeStruct((16, ch), F32)),
        scratch_shapes=[pltpu.VMEM((2, times, width, count), BF16)],
        compiler_params=pltpu.CompilerParams(vmem_limit_bytes=VMEM_LIMIT),
        cost_estimate=pl.CostEstimate(
            flops=times * count * ch * ch * 96, bytes_accessed=12 << 20, transcendentals=0
        ),
        name="grads",
    )(place, states, adjoints, state_in, adjoint_in, log_decay, frame_taps, cot_taps)


def output_kernel(place, field, first, second, weight, skip, direct, out, pairs, blocks, *, flip):
    times, half, cols, width = field.shape
    ch = width // 2
    fill_weights(blocks, weight, flip)
    top, bottom = pick_halos(first, second, int(flip), lax.rem(place[0], 2) == 1, times)
    fill_pairs_from_pairs(pairs, field, top, bottom)
    gain = skip[...]
    for t in range(times):
        taps = column_taps(pairs[t].reshape((half + 1) * cols, width), cols)
        value = conv_pairs(taps, blocks, half * cols, cols, flip).reshape(half, cols, width)
        for i in range(half):
            for c in range(2):
                base = gain * direct[t, 2 * i + c].astype(F32)
                out[t, 2 * i + c] = (value[i, :, c * ch : (c + 1) * ch] + base).astype(BF16)


def output_call(place, field, first, second, weight, skip, direct, flip):
    times, half, cols, width = field.shape
    ch = width // 2
    return pl.pallas_call(
        functools.partial(output_kernel, flip=flip),
        in_specs=[pl.BlockSpec(memory_space=pltpu.SMEM)]
        + [pl.BlockSpec(memory_space=pltpu.VMEM)] * 6,
        out_shape=jax.ShapeDtypeStruct(direct.shape, BF16),
        scratch_shapes=[
            pltpu.VMEM((times, half + 1, cols, width), BF16),
            pltpu.VMEM((3, 2, width, width), BF16),
        ],
        compiler_params=pltpu.CompilerParams(vmem_limit_bytes=VMEM_LIMIT),
        cost_estimate=pl.CostEstimate(
            flops=times * half * cols * ch * ch * 48, bytes_accessed=4 << 20, transcendentals=0
        ),
        name="grad_frames" if flip else "output",
    )(place, field, first, second, weight, skip, direct)


def swap(value, tm_bits, tile_bits):
    tiles = lax.axis_size("tile")
    mask = tm_bits * tiles + tile_bits
    count = lax.axis_size("tm") * tiles
    return lax.ppermute(value, ("tm", "tile"), [(i, i ^ mask) for i in range(count)])


def swap_across(value):
    count = lax.axis_size("tile")
    pairs = []
    for i in range(1, count - 1, 2):
        pairs += [(i, i + 1), (i + 1, i)]
    return lax.ppermute(value, "tile", pairs)


def laid(parts, count):
    total, start = None, 0
    for part in parts:
        end = count - start - part.shape[0]
        wide = jnp.pad(part, ((start, end), (0, 0)))
        total = wide if total is None else total + wide
        start += part.shape[0]
    return total


def packed(value, scale, *rows):
    parts = [value * jnp.exp2(-scale), *rows]
    return laid(parts, value.shape[0] + 16).astype(jnp.float16)


def whole_decay(rows):
    return rows[0:1] + rows[1:2] / 256.0 + rows[2:3] / 65536.0


def by_place(values, flags):
    values = list(values)
    for n, flag in enumerate(flags):
        for d in range(len(values)):
            if not d >> n & 1:
                a, b = values[d], values[d + 2**n]
                values[d], values[d + 2**n] = jnp.where(flag, b, a), jnp.where(flag, a, b)
    return values


def carry_over(state_end, adjoint_end, info):
    squares = lax.axis_size("tm") // 4
    flags = [info[5:6] > 0.5, info[6:7] > 0.5]
    places = [info[7 + d : 8 + d] for d in range(squares)]
    part = state_end.shape[0] // 4
    width = state_end.shape[1]

    def both(low, high, scale_low, scale_high, rows):
        parts = [low * jnp.exp2(-scale_low), high * jnp.exp2(-scale_high), rows]
        return laid(parts, 2 * part + 16).astype(jnp.float16)

    def quarters(value):
        return by_place([value[n * part : (n + 1) * part] for n in range(4)], flags)

    states, adjoints = quarters(state_end), quarters(adjoint_end)
    messages = [both(states[d], adjoints[d], info[0:1], info[1:2], info[:5]) for d in (1, 2, 3)]
    received = [swap(m, d + 1, 0).astype(F32) for d, m in enumerate(messages)]
    rows = [info[:5]] + [got[2 * part : 2 * part + 5] for got in received]
    state_scale = functools.reduce(jnp.maximum, [row[0:1] for row in rows])
    adjoint_scale = functools.reduce(jnp.maximum, [row[1:2] for row in rows])
    states = [states[0]] + [
        got[:part] * jnp.exp2(row[0:1]) for got, row in zip(received, rows[1:])
    ]
    adjoints = [adjoints[0]] + [
        got[part : 2 * part] * jnp.exp2(row[1:2]) for got, row in zip(received, rows[1:])
    ]
    states, adjoints = by_place(states, flags), by_place(adjoints, flags)
    decay_rows = by_place([row[2:5] for row in rows], flags)
    totals = [whole_decay(row) for row in decay_rows]

    one = jnp.ones((1, width), F32)
    zero = jnp.zeros((part, width), F32)
    before, reach = [zero], [one]
    for n in range(4):
        before.append(totals[n] * before[-1] + states[n])
        reach.append(reach[-1] * totals[n])
    after, back = [zero], [one]
    for n in (3, 2, 1, 0):
        after.insert(0, adjoints[n] + totals[n] * after[0])
        back.insert(0, back[0] * totals[n])
    state_square, adjoint_square = before.pop(), after.pop(0)
    back.pop(0)

    messages = []
    bit = 1
    while bit < squares:
        later = places[bit] < places[0]
        scale = jnp.where(later, adjoint_scale, state_scale)
        value = jnp.where(later, adjoint_square, state_square)
        messages.append(packed(value, scale, scale, *decay_rows))
        bit *= 2
    through_square, values = {}, {}
    top_scale = jnp.maximum(state_scale, adjoint_scale)
    for d in range(1, squares):
        got = swap(messages[d.bit_length() - 1], 4 * d, 0).astype(F32)
        there = [got[part + 1 + 3 * n : part + 4 + 3 * n] for n in range(4)]
        through_square[d] = functools.reduce(jnp.multiply, [whole_decay(row) for row in there])
        values[d] = got[:part] * jnp.exp2(got[part : part + 1])
        top_scale = jnp.maximum(top_scale, got[part : part + 1])
    state_before, adjoint_after = zero, zero
    for d in values:
        term = values[d]
        if squares > 2:
            through = one
            for e in values:
                low = jnp.minimum(places[0], places[d])
                high = jnp.maximum(places[0], places[d])
                inside = (low < places[e]) & (places[e] < high)
                through = through * jnp.where(inside, through_square[e], 1.0)
            term = through * term
        state_before = state_before + jnp.where(places[d] < places[0], term, 0.0)
        adjoint_after = adjoint_after + jnp.where(places[d] > places[0], term, 0.0)

    states = by_place([before[n] + reach[n] * state_before for n in range(4)], flags)
    adjoints = by_place([after[n] + back[n] * adjoint_after for n in range(4)], flags)
    messages = [both(states[d], adjoints[d], top_scale, top_scale, top_scale) for d in (1, 2, 3)]
    received = [swap(m, d + 1, 0).astype(F32) for d, m in enumerate(messages)]
    scales = [jnp.exp2(got[2 * part : 2 * part + 1]) for got in received]
    states = [states[0]] + [got[:part] * s for got, s in zip(received, scales)]
    adjoints = [adjoints[0]] + [got[part : 2 * part] * s for got, s in zip(received, scales)]
    return (
        jnp.concatenate(by_place(states, flags), 0),
        jnp.concatenate(by_place(adjoints, flags), 0),
    )


def unpacked(got):
    rows = got.shape[-2] - 16
    wide = got.astype(F32)
    scale = wide[..., rows : rows + 1, :]
    return wide[..., :rows, :] * jnp.exp2(scale), scale


def shards(frames, cotangent, w_in, w_out, skip, log_decay):
    times, rows, cols, ch = frames.shape
    half = rows // 2
    place = jnp.stack([lax.axis_index("tile"), lax.axis_index("tm")]).astype(jnp.int32)
    place = lax.optimization_barrier(place)
    odd = place[0] % 2 == 1
    gain = skip[None, :]

    low = jnp.stack([frames[:, 0], cotangent[:, 0]])
    high = jnp.stack([frames[:, -1], cotangent[:, -1]])
    second = swap_across(jnp.where(odd, high, low))
    first = swap(jnp.where(odd, low, high), 0, 1)

    fields = jnp.stack([frames, cotangent])
    blocks = blocks_call(fields, jnp.stack([w_in, w_out]), log_decay)
    states, adjoints, leaving, frame_taps, cot_taps, info = drive_call(
        place, fields, first, second, blocks, log_decay
    )
    state_in, adjoint_in = carry_over(states[-1], leaving, info)
    states_bf, inflow_bf, first, second, in_part, out_part, info = grads_call(
        place, states, adjoints, state_in, adjoint_in, log_decay, frame_taps, cot_taps
    )

    out_scale, in_scale = info[0:1], info[1:2]
    odd, odd_tm, high_tile = (info[n : n + 1] > 0.5 for n in (2, 3, 4))
    scale = jnp.where(odd, in_scale, out_scale)
    message = packed(jnp.where(odd, in_part, out_part), scale, scale)
    message, first, second = lax.optimization_barrier((message, first, second))
    got, got_scale = unpacked(swap(message, 0, 1))
    value = jnp.where(odd, out_part, in_part) + got
    scale = jnp.maximum(jnp.where(odd, out_scale, in_scale), got_scale)
    second = swap_across(second)
    first = swap(first, 0, 1)

    bits = [((1, 0), odd_tm), ((0, 2), high_tile)] if lax.axis_size("tile") > 2 else [((1, 0), odd_tm)]
    parts = 2 ** len(bits)
    pieces = list(value.reshape(parts, -1, ch))
    for n, (_, high) in enumerate(bits):
        for d in range(parts):
            if not d >> n & 1:
                a, b = pieces[d], pieces[d + 2**n]
                pieces[d], pieces[d + 2**n] = jnp.where(high, b, a), jnp.where(high, a, b)

    def mask(d):
        chosen = [bit for n, (bit, _) in enumerate(bits) if d >> n & 1]
        return sum(b[0] for b in chosen), sum(b[1] for b in chosen)

    messages = [packed(pieces[d], scale, scale) for d in range(1, parts)]
    value = pieces[0]
    states_bf = states_bf.reshape(times, half, cols, 2 * ch)
    inflow_bf = inflow_bf.reshape(times, half, cols, 2 * ch)
    *messages, states_bf = lax.optimization_barrier((*messages, states_bf))
    received = [swap(m, *mask(d + 1)) for d, m in enumerate(messages)]
    output = output_call(place, states_bf, first, second, w_out, gain, frames, False)
    for got in received:
        got, got_scale = unpacked(got)
        value = value + got
        scale = jnp.maximum(scale, got_scale)

    left = []
    bit = 2
    while bit < lax.axis_size("tm"):
        left.append((bit, 0))
        bit *= 2
    bit = 4
    while bit < lax.axis_size("tile"):
        left.append((0, bit))
        bit *= 2
    waiting = inflow_bf
    for n in range(0, len(left), 2):
        group = left[n : n + 2]
        message = packed(value, scale, scale)
        message, output, waiting = lax.optimization_barrier((message, output, waiting))
        terms = [message]
        for d in range(1, 2 ** len(group)):
            chosen = [b for k, b in enumerate(group) if d >> k & 1]
            terms.append(swap(message, sum(b[0] for b in chosen), sum(b[1] for b in chosen)))
        terms = [unpacked(term) for term in terms]
        while len(terms) > 1:
            terms = [
                (a[0] + b[0], jnp.maximum(a[1], b[1])) for a, b in zip(terms[::2], terms[1::2])
            ]
        value, scale = terms[0]
    grad_frames = output_call(place, waiting, first, second, w_in, gain, cotangent, True)

    message = packed(value, scale, scale)
    message, grad_frames = lax.optimization_barrier((message, grad_frames))
    gathered = [message] + [swap(message, *mask(d)) for d in range(1, parts)]
    for _, high in bits:
        gathered = [
            (jnp.where(high, b, a), jnp.where(high, a, b))
            for a, b in zip(gathered[::2], gathered[1::2])
        ]
        gathered = [jnp.concatenate(pair, 0) for pair in gathered]
    (mine,) = gathered
    mine = lax.optimization_barrier(mine)
    theirs = swap(mine, 0, 1)
    factor = 1.0 / math.sqrt(
        times * lax.axis_size("tm") * rows * lax.axis_size("tile") * cols
    )
    results = []
    for chosen in (jnp.where(odd, theirs, mine), jnp.where(odd, mine, theirs)):
        whole, _ = unpacked(chosen.reshape(parts, -1, ch))
        results.append((whole * factor).reshape(3, 3, ch, ch))
    return (output, grad_frames, results[0], results[1])


def solution(mesh):
    placed = (
        P("tm", "tile", None, None),
        P("tm", "tile", None, None),
        P(),
        P(),
        P(),
        P("tm", None),
    )
    return jax.shard_map(
        shards,
        mesh=mesh,
        in_specs=placed,
        out_specs=(P("tm", "tile", None, None), P("tm", "tile", None, None), P(), P()),
        check_vma=False,
    )
```

```python
import functools
import math

import jax
import jax.numpy as jnp
from jax import lax
from jax.experimental import pallas as pl
from jax.experimental.pallas import tpu as pltpu
from jax.sharding import PartitionSpec as P

F32 = jnp.float32
BF16 = jnp.bfloat16
VMEM_LIMIT = 24 * 1024 * 1024


def fill_pairs(pairs, field, top, bottom):
    half = field.shape[1] // 2
    ch = field.shape[3]
    pairs[:, 0, :, :ch] = top[:, 0]
    pairs[:, half, :, ch:] = bottom[:, 0]
    for i in range(half):
        pairs[:, i, :, ch:] = field[:, 2 * i]
        pairs[:, i + 1, :, :ch] = field[:, 2 * i + 1]


def fill_pairs_from_pairs(pairs, field, top, bottom):
    half = field.shape[1]
    ch = field.shape[3] // 2
    pairs[:, 0, :, :ch] = top[:, 0]
    pairs[:, half, :, ch:] = bottom[:, 0]
    pairs[:, :half, :, ch:] = field[:, :, :, :ch]
    pairs[:, 1:, :, :ch] = field[:, :, :, ch:]


def column_taps(flat, cols):
    wide = flat.astype(F32)
    count = wide.shape[0]
    col = lax.broadcasted_iota(jnp.int32, wide.shape, 0) % cols
    left = jnp.where(col == 0, 0.0, pltpu.roll(wide, 1, 0)).astype(flat.dtype)
    right = jnp.where(col == cols - 1, 0.0, pltpu.roll(wide, count - 1, 0)).astype(flat.dtype)
    return left, flat, right


def fill_weights(blocks, weight, flip):
    ch = weight.shape[2]
    zero = jnp.zeros((ch, ch), weight.dtype)
    for j in range(3):
        for b in range(2):
            for k in range(2):
                for n in range(2):
                    tap = 2 * b + k - n
                    ok = 0 <= tap <= 2
                    if flip:
                        value = weight[2 - tap, 2 - j] if ok else zero
                        blocks[j, b, n * ch : (n + 1) * ch, k * ch : (k + 1) * ch] = value
                    else:
                        value = weight[tap, j] if ok else zero
                        blocks[j, b, k * ch : (k + 1) * ch, n * ch : (n + 1) * ch] = value


def conv_pairs(taps, blocks, rows_out, cols, flip):
    dims = (((1,), (1,)), ((), ())) if flip else (((1,), (0,)), ((), ()))
    total = None
    for j in range(3):
        for b in range(2):
            part = lax.dot_general(
                taps[j][b * cols : b * cols + rows_out],
                blocks[j, b],
                dims,
                preferred_element_type=F32,
            )
            total = part if total is None else total + part
    return total


def pick_halos(first, second, index, odd, times):
    one = first[index].astype(F32)
    two = second[index].astype(F32)
    upper = jnp.where(odd, one, two).astype(BF16)
    lower = jnp.where(odd, two, one).astype(BF16)
    return upper[:, None], lower[:, None]


def exponent(value):
    top = jnp.max(jnp.abs(value), axis=0, keepdims=True)
    return jnp.ceil(jnp.log2(jnp.maximum(top, 1e-30)))


def decays(log_decay):
    wide = jnp.concatenate([log_decay, log_decay], 1)
    times = wide.shape[0]
    sums = [wide[0:1]]
    for t in range(1, times):
        sums.append(sums[-1] + wide[t : t + 1])
    rate = [jnp.exp(wide[t : t + 1]) for t in range(times)]
    reach = [jnp.exp(total) for total in sums]
    tail = [jnp.exp(sums[-1] - total) for total in sums]
    return rate, reach, tail


def blocks_kernel(fields, weights, log_decay, blocks):
    fill_weights(blocks.at[0], weights.at[0], False)
    fill_weights(blocks.at[1], weights.at[1], True)


def blocks_call(fields, weights, log_decay):
    ch = weights.shape[3]
    return pl.pallas_call(
        blocks_kernel,
        out_shape=jax.ShapeDtypeStruct((2, 3, 2, 2 * ch, 2 * ch), BF16),
        compiler_params=pltpu.CompilerParams(vmem_limit_bytes=VMEM_LIMIT),
        cost_estimate=pl.CostEstimate(flops=0, bytes_accessed=10 << 20, transcendentals=0),
        name="blocks",
    )(fields, weights, log_decay)


def drive_kernel(
    place,
    fields,
    first,
    second,
    blocks,
    log_decay,
    states,
    adjoints,
    leaving,
    frame_taps,
    cot_taps,
    info,
    pairs,
):
    _, times, rows, cols, ch = fields.shape
    half = rows // 2
    odd = lax.rem(place[0], 2) == 1
    rate, reach, _ = decays(log_decay[...])
    results = ((states, frame_taps), (adjoints, cot_taps))
    for index, (result, taps_out) in enumerate(results):
        flip = index == 1
        top, bottom = pick_halos(first, second, index, odd, times)
        fill_pairs(pairs.at[index], fields.at[index], top, bottom)
        carry = None
        for step in range(times):
            t = times - 1 - step if flip else step
            taps = column_taps(pairs[index, t].reshape((half + 1) * cols, 2 * ch), cols)
            for j in range(3):
                taps_out[j, t] = taps[j]
            value = conv_pairs(taps, blocks.at[index], half * cols, cols, flip)
            if flip:
                value = value if carry is None else value + carry
                carry = rate[t] * value
            else:
                value = (1.0 - rate[t]) * value
                value = value if carry is None else rate[t] * carry + value
                carry = value
            result[t] = value
        if flip:
            leaving[...] = carry
        info[index : index + 1, :] = exponent(carry)
    total = reach[-1]
    high = total.astype(BF16).astype(F32)
    rest = (total - high) * 256.0
    middle = rest.astype(BF16).astype(F32)
    low = ((rest - middle) * 256.0).astype(BF16).astype(F32)
    info[2:3, :] = high
    info[3:4, :] = middle
    info[4:5, :] = low
    row = jnp.zeros((1, 2 * ch), F32)
    info[5:6, :] = row + lax.rem(place[1], 2).astype(F32)
    info[6:7, :] = row + lax.rem(lax.div(place[1], 2), 2).astype(F32)
    for d in range(info.shape[0] - 7):
        info[7 + d : 8 + d, :] = row + (lax.div(place[1], 4) ^ d).astype(F32)


def drive_call(place, fields, first, second, blocks, log_decay):
    _, times, rows, cols, ch = fields.shape
    half = rows // 2
    field = jax.ShapeDtypeStruct((times, half * cols, 2 * ch), F32)
    rows_info = (7 + lax.axis_size("tm") // 4 + 15) // 16 * 16
    taps = jax.ShapeDtypeStruct((3, times, (half + 1) * cols, 2 * ch), BF16)
    return pl.pallas_call(
        drive_kernel,
        in_specs=[pl.BlockSpec(memory_space=pltpu.SMEM)]
        + [pl.BlockSpec(memory_space=pltpu.VMEM)] * 5,
        out_shape=(
            field,
            field,
            jax.ShapeDtypeStruct(field.shape[1:], F32),
            taps,
            taps,
            jax.ShapeDtypeStruct((rows_info, 2 * ch), F32),
        ),
        scratch_shapes=[
            pltpu.VMEM((2, times, half + 1, cols, 2 * ch), BF16),
        ],
        compiler_params=pltpu.CompilerParams(vmem_limit_bytes=VMEM_LIMIT),
        cost_estimate=pl.CostEstimate(
            flops=times * rows * cols * ch * ch * 48, bytes_accessed=12 << 20, transcendentals=0
        ),
        name="drive",
    )(place, fields, first, second, blocks, log_decay)


def grads_kernel(
    place,
    states,
    adjoints,
    state_in,
    adjoint_in,
    log_decay,
    frame_taps,
    cot_taps,
    states_bf,
    inflow_bf,
    first,
    second,
    grads_in,
    grads_out,
    info,
    turned,
):
    times, count, width = states.shape
    ch = width // 2
    cols = frame_taps.shape[2] - count
    odd = lax.rem(place[0], 2) == 1
    rate, reach, tail = decays(log_decay[...])
    add = state_in[...]
    back = adjoint_in[...]
    for t in range(times):
        value = (states[t] + reach[t] * add).astype(BF16)
        states_bf[t] = value
        turned[0, t] = value.T
        value = ((1.0 - rate[t]) * (adjoints[t] + tail[t] * back)).astype(BF16)
        inflow_bf[t] = value
        turned[1, t] = value.T
        for index, field in enumerate((states_bf, inflow_bf)):
            low = field[t, :cols, :ch].astype(F32)
            high = field[t, count - cols :, ch:].astype(F32)
            first[index, t] = jnp.where(odd, low, high).astype(BF16)
            second[index, t] = jnp.where(odd, high, low).astype(BF16)
    for index, (taps, grads) in enumerate(((cot_taps, grads_out), (frame_taps, grads_in))):
        largest = None
        for j in range(3):
            blocks = []
            for b in range(2):
                total = None
                for t in range(times):
                    part = jnp.dot(
                        turned[index, t],
                        taps[j, t, b * cols : b * cols + count],
                        preferred_element_type=F32,
                    )
                    total = part if total is None else total + part
                blocks.append(total)
            for tap in range(3):
                total = None
                for b in range(2):
                    for c in range(2):
                        a = 2 * b + c - tap
                        if a in (0, 1):
                            part = blocks[b][a * ch : (a + 1) * ch, c * ch : (c + 1) * ch]
                            total = part if total is None else total + part
                if index == 0:
                    spot = (2 - tap) * 3 + 2 - j
                else:
                    spot = tap * 3 + j
                    total = total.T
                grads[spot * ch : (spot + 1) * ch, :] = total
                top = jnp.max(jnp.abs(total), axis=0, keepdims=True)
                largest = top if largest is None else jnp.maximum(largest, top)
        info[index : index + 1, :] = exponent(largest)
    row = jnp.zeros((1, ch), F32)
    info[2:3, :] = row + lax.rem(place[0], 2).astype(F32)
    info[3:4, :] = row + lax.rem(place[1], 2).astype(F32)
    info[4:5, :] = row + lax.rem(lax.div(place[0], 2), 2).astype(F32)
    info[5:, :] = jnp.zeros((info.shape[0] - 5, ch), F32)


def grads_call(place, states, adjoints, state_in, adjoint_in, log_decay, frame_taps, cot_taps):
    times, count, width = states.shape
    ch = width // 2
    cols = frame_taps.shape[2] - count
    field = jax.ShapeDtypeStruct((times, count, width), BF16)
    edge = jax.ShapeDtypeStruct((2, times, cols, ch), BF16)
    grads = jax.ShapeDtypeStruct((9 * ch, ch), F32)
    return pl.pallas_call(
        grads_kernel,
        in_specs=[pl.BlockSpec(memory_space=pltpu.SMEM)]
        + [pl.BlockSpec(memory_space=pltpu.VMEM)] * 7,
        out_shape=(field, field, edge, edge, grads, grads, jax.ShapeDtypeStruct((16, ch), F32)),
        scratch_shapes=[pltpu.VMEM((2, times, width, count), BF16)],
        compiler_params=pltpu.CompilerParams(vmem_limit_bytes=VMEM_LIMIT),
        cost_estimate=pl.CostEstimate(
            flops=times * count * ch * ch * 96, bytes_accessed=12 << 20, transcendentals=0
        ),
        name="grads",
    )(place, states, adjoints, state_in, adjoint_in, log_decay, frame_taps, cot_taps)


def output_kernel(place, field, first, second, weight, skip, direct, out, pairs, blocks, *, flip):
    times, half, cols, width = field.shape
    ch = width // 2
    fill_weights(blocks, weight, flip)
    top, bottom = pick_halos(first, second, int(flip), lax.rem(place[0], 2) == 1, times)
    fill_pairs_from_pairs(pairs, field, top, bottom)
    gain = skip[...]
    for t in range(times):
        taps = column_taps(pairs[t].reshape((half + 1) * cols, width), cols)
        value = conv_pairs(taps, blocks, half * cols, cols, flip).reshape(half, cols, width)
        for i in range(half):
            for c in range(2):
                base = gain * direct[t, 2 * i + c].astype(F32)
                out[t, 2 * i + c] = (value[i, :, c * ch : (c + 1) * ch] + base).astype(BF16)


def output_call(place, field, first, second, weight, skip, direct, flip):
    times, half, cols, width = field.shape
    ch = width // 2
    return pl.pallas_call(
        functools.partial(output_kernel, flip=flip),
        in_specs=[pl.BlockSpec(memory_space=pltpu.SMEM)]
        + [pl.BlockSpec(memory_space=pltpu.VMEM)] * 6,
        out_shape=jax.ShapeDtypeStruct(direct.shape, BF16),
        scratch_shapes=[
            pltpu.VMEM((times, half + 1, cols, width), BF16),
            pltpu.VMEM((3, 2, width, width), BF16),
        ],
        compiler_params=pltpu.CompilerParams(vmem_limit_bytes=VMEM_LIMIT),
        cost_estimate=pl.CostEstimate(
            flops=times * half * cols * ch * ch * 48, bytes_accessed=4 << 20, transcendentals=0
        ),
        name="grad_frames" if flip else "output",
    )(place, field, first, second, weight, skip, direct)


def swap(value, tm_bits, tile_bits):
    tiles = lax.axis_size("tile")
    mask = tm_bits * tiles + tile_bits
    count = lax.axis_size("tm") * tiles
    return lax.ppermute(value, ("tm", "tile"), [(i, i ^ mask) for i in range(count)])


def swap_across(value):
    count = lax.axis_size("tile")
    pairs = []
    for i in range(1, count - 1, 2):
        pairs += [(i, i + 1), (i + 1, i)]
    return lax.ppermute(value, "tile", pairs)


def laid(parts, count):
    total, start = None, 0
    for part in parts:
        end = count - start - part.shape[0]
        wide = jnp.pad(part, ((start, end), (0, 0)))
        total = wide if total is None else total + wide
        start += part.shape[0]
    return total


def packed(value, scale, *rows):
    parts = [value * jnp.exp2(-scale), *rows]
    return laid(parts, value.shape[0] + 16).astype(jnp.float16)


def whole_decay(rows):
    return rows[0:1] + rows[1:2] / 256.0 + rows[2:3] / 65536.0


def by_place(values, flags):
    values = list(values)
    for n, flag in enumerate(flags):
        for d in range(len(values)):
            if not d >> n & 1:
                a, b = values[d], values[d + 2**n]
                values[d], values[d + 2**n] = jnp.where(flag, b, a), jnp.where(flag, a, b)
    return values


def carry_over(state_end, adjoint_end, info):
    squares = lax.axis_size("tm") // 4
    flags = [info[5:6] > 0.5, info[6:7] > 0.5]
    places = [info[7 + d : 8 + d] for d in range(squares)]
    part = state_end.shape[0] // 4
    width = state_end.shape[1]

    def both(low, high, scale_low, scale_high, rows):
        parts = [low * jnp.exp2(-scale_low), high * jnp.exp2(-scale_high), rows]
        return laid(parts, 2 * part + 16).astype(jnp.float16)

    def quarters(value):
        return by_place([value[n * part : (n + 1) * part] for n in range(4)], flags)

    states, adjoints = quarters(state_end), quarters(adjoint_end)
    messages = [both(states[d], adjoints[d], info[0:1], info[1:2], info[:5]) for d in (1, 2, 3)]
    received = [swap(m, d + 1, 0).astype(F32) for d, m in enumerate(messages)]
    rows = [info[:5]] + [got[2 * part : 2 * part + 5] for got in received]
    state_scale = functools.reduce(jnp.maximum, [row[0:1] for row in rows])
    adjoint_scale = functools.reduce(jnp.maximum, [row[1:2] for row in rows])
    states = [states[0]] + [
        got[:part] * jnp.exp2(row[0:1]) for got, row in zip(received, rows[1:])
    ]
    adjoints = [adjoints[0]] + [
        got[part : 2 * part] * jnp.exp2(row[1:2]) for got, row in zip(received, rows[1:])
    ]
    states, adjoints = by_place(states, flags), by_place(adjoints, flags)
    decay_rows = by_place([row[2:5] for row in rows], flags)
    totals = [whole_decay(row) for row in decay_rows]

    one = jnp.ones((1, width), F32)
    zero = jnp.zeros((part, width), F32)
    before, reach = [zero], [one]
    for n in range(4):
        before.append(totals[n] * before[-1] + states[n])
        reach.append(reach[-1] * totals[n])
    after, back = [zero], [one]
    for n in (3, 2, 1, 0):
        after.insert(0, adjoints[n] + totals[n] * after[0])
        back.insert(0, back[0] * totals[n])
    state_square, adjoint_square = before.pop(), after.pop(0)
    back.pop(0)

    messages = []
    bit = 1
    while bit < squares:
        later = places[bit] < places[0]
        scale = jnp.where(later, adjoint_scale, state_scale)
        value = jnp.where(later, adjoint_square, state_square)
        messages.append(packed(value, scale, scale, *decay_rows))
        bit *= 2
    through_square, values = {}, {}
    top_scale = jnp.maximum(state_scale, adjoint_scale)
    for d in range(1, squares):
        got = swap(messages[d.bit_length() - 1], 4 * d, 0).astype(F32)
        there = [got[part + 1 + 3 * n : part + 4 + 3 * n] for n in range(4)]
        through_square[d] = functools.reduce(jnp.multiply, [whole_decay(row) for row in there])
        values[d] = got[:part] * jnp.exp2(got[part : part + 1])
        top_scale = jnp.maximum(top_scale, got[part : part + 1])
    state_before, adjoint_after = zero, zero
    for d in values:
        term = values[d]
        if squares > 2:
            through = one
            for e in values:
                low = jnp.minimum(places[0], places[d])
                high = jnp.maximum(places[0], places[d])
                inside = (low < places[e]) & (places[e] < high)
                through = through * jnp.where(inside, through_square[e], 1.0)
            term = through * term
        state_before = state_before + jnp.where(places[d] < places[0], term, 0.0)
        adjoint_after = adjoint_after + jnp.where(places[d] > places[0], term, 0.0)

    states = by_place([before[n] + reach[n] * state_before for n in range(4)], flags)
    adjoints = by_place([after[n] + back[n] * adjoint_after for n in range(4)], flags)
    messages = [both(states[d], adjoints[d], top_scale, top_scale, top_scale) for d in (1, 2, 3)]
    received = [swap(m, d + 1, 0).astype(F32) for d, m in enumerate(messages)]
    scales = [jnp.exp2(got[2 * part : 2 * part + 1]) for got in received]
    states = [states[0]] + [got[:part] * s for got, s in zip(received, scales)]
    adjoints = [adjoints[0]] + [got[part : 2 * part] * s for got, s in zip(received, scales)]
    return (
        jnp.concatenate(by_place(states, flags), 0),
        jnp.concatenate(by_place(adjoints, flags), 0),
    )


def unpacked(got):
    rows = got.shape[-2] - 16
    wide = got.astype(F32)
    scale = wide[..., rows : rows + 1, :]
    return wide[..., :rows, :] * jnp.exp2(scale), scale


def shards(frames, cotangent, w_in, w_out, skip, log_decay):
    times, rows, cols, ch = frames.shape
    half = rows // 2
    place = jnp.stack([lax.axis_index("tile"), lax.axis_index("tm")]).astype(jnp.int32)
    place = lax.optimization_barrier(place)
    odd = place[0] % 2 == 1
    gain = skip[None, :]

    low = jnp.stack([frames[:, 0], cotangent[:, 0]])
    high = jnp.stack([frames[:, -1], cotangent[:, -1]])
    second = swap_across(jnp.where(odd, high, low))
    first = swap(jnp.where(odd, low, high), 0, 1)

    fields = jnp.stack([frames, cotangent])
    blocks = blocks_call(fields, jnp.stack([w_in, w_out]), log_decay)
    states, adjoints, leaving, frame_taps, cot_taps, info = drive_call(
        place, fields, first, second, blocks, log_decay
    )
    state_in, adjoint_in = carry_over(states[-1], leaving, info)
    states_bf, inflow_bf, first, second, in_part, out_part, info = grads_call(
        place, states, adjoints, state_in, adjoint_in, log_decay, frame_taps, cot_taps
    )

    out_scale, in_scale = info[0:1], info[1:2]
    odd, odd_tm, high_tile = (info[n : n + 1] > 0.5 for n in (2, 3, 4))
    scale = jnp.where(odd, in_scale, out_scale)
    message = packed(jnp.where(odd, in_part, out_part), scale, scale)
    message, first, second = lax.optimization_barrier((message, first, second))
    got, got_scale = unpacked(swap(message, 0, 1))
    value = jnp.where(odd, out_part, in_part) + got
    scale = jnp.maximum(jnp.where(odd, out_scale, in_scale), got_scale)
    second = swap_across(second)
    first = swap(first, 0, 1)

    bits = [((1, 0), odd_tm), ((0, 2), high_tile)] if lax.axis_size("tile") > 2 else [((1, 0), odd_tm)]
    parts = 2 ** len(bits)
    pieces = list(value.reshape(parts, -1, ch))
    for n, (_, high) in enumerate(bits):
        for d in range(parts):
            if not d >> n & 1:
                a, b = pieces[d], pieces[d + 2**n]
                pieces[d], pieces[d + 2**n] = jnp.where(high, b, a), jnp.where(high, a, b)

    def mask(d):
        chosen = [bit for n, (bit, _) in enumerate(bits) if d >> n & 1]
        return sum(b[0] for b in chosen), sum(b[1] for b in chosen)

    messages = [packed(pieces[d], scale, scale) for d in range(1, parts)]
    value = pieces[0]
    states_bf = states_bf.reshape(times, half, cols, 2 * ch)
    inflow_bf = inflow_bf.reshape(times, half, cols, 2 * ch)
    *messages, states_bf = lax.optimization_barrier((*messages, states_bf))
    received = [swap(m, *mask(d + 1)) for d, m in enumerate(messages)]
    for got in received:
        got, got_scale = unpacked(got)
        value = value + got
        scale = jnp.maximum(scale, got_scale)

    left = []
    bit = 2
    while bit < lax.axis_size("tm"):
        left.append((bit, 0))
        bit *= 2
    bit = 4
    while bit < lax.axis_size("tile"):
        left.append((0, bit))
        bit *= 2
    waiting = inflow_bf
    for n in range(0, len(left), 2):
        group = left[n : n + 2]
        message = packed(value, scale, scale)
        message, states_bf, waiting = lax.optimization_barrier((message, states_bf, waiting))
        terms = [message]
        for d in range(1, 2 ** len(group)):
            chosen = [b for k, b in enumerate(group) if d >> k & 1]
            terms.append(swap(message, sum(b[0] for b in chosen), sum(b[1] for b in chosen)))
        terms = [unpacked(term) for term in terms]
        while len(terms) > 1:
            terms = [
                (a[0] + b[0], jnp.maximum(a[1], b[1])) for a, b in zip(terms[::2], terms[1::2])
            ]
        value, scale = terms[0]

    output = output_call(place, states_bf, first, second, w_out, gain, frames, False)

    message = packed(value, scale, scale)
    message, output, waiting = lax.optimization_barrier((message, output, waiting))
    gathered = [message] + [swap(message, *mask(d)) for d in range(1, parts)]
    grad_frames = output_call(place, waiting, first, second, w_in, gain, cotangent, True)
    for _, high in bits:
        gathered = [
            (jnp.where(high, b, a), jnp.where(high, a, b))
            for a, b in zip(gathered[::2], gathered[1::2])
        ]
        gathered = [jnp.concatenate(pair, 0) for pair in gathered]
    (mine,) = gathered
    mine, grad_frames = lax.optimization_barrier((mine, grad_frames))
    theirs = swap(mine, 0, 1)
    factor = 1.0 / math.sqrt(
        times * lax.axis_size("tm") * rows * lax.axis_size("tile") * cols
    )
    mine, _ = unpacked(mine.reshape(parts, -1, ch))
    theirs, _ = unpacked(theirs.reshape(parts, -1, ch))
    results = [
        (jnp.where(odd, a, b) * factor).reshape(3, 3, ch, ch)
        for a, b in ((theirs, mine), (mine, theirs))
    ]
    return (output, grad_frames, results[0], results[1])


def solution(mesh):
    placed = (
        P("tm", "tile", None, None),
        P("tm", "tile", None, None),
        P(),
        P(),
        P(),
        P("tm", None),
    )
    return jax.shard_map(
        shards,
        mesh=mesh,
        in_specs=placed,
        out_specs=(P("tm", "tile", None, None), P("tm", "tile", None, None), P(), P()),
        check_vma=False,
    )
```

```python
import functools
import math

import jax
import jax.numpy as jnp
from jax import lax
from jax.experimental import pallas as pl
from jax.experimental.pallas import tpu as pltpu
from jax.sharding import PartitionSpec as P

F32 = jnp.float32
BF16 = jnp.bfloat16
VMEM_LIMIT = 24 * 1024 * 1024


def fill_pairs(pairs, field, top, bottom):
    half = field.shape[1] // 2
    ch = field.shape[3]
    pairs[:, 0, :, :ch] = top[:, 0]
    pairs[:, half, :, ch:] = bottom[:, 0]
    for i in range(half):
        pairs[:, i, :, ch:] = field[:, 2 * i]
        pairs[:, i + 1, :, :ch] = field[:, 2 * i + 1]


def fill_pairs_from_pairs(pairs, field, top, bottom):
    half = field.shape[1]
    ch = field.shape[3] // 2
    pairs[:, 0, :, :ch] = top[:, 0]
    pairs[:, half, :, ch:] = bottom[:, 0]
    pairs[:, :half, :, ch:] = field[:, :, :, :ch]
    pairs[:, 1:, :, :ch] = field[:, :, :, ch:]


def column_taps(flat, cols):
    wide = flat.astype(F32)
    count = wide.shape[0]
    col = lax.broadcasted_iota(jnp.int32, wide.shape, 0) % cols
    left = jnp.where(col == 0, 0.0, pltpu.roll(wide, 1, 0)).astype(flat.dtype)
    right = jnp.where(col == cols - 1, 0.0, pltpu.roll(wide, count - 1, 0)).astype(flat.dtype)
    return left, flat, right


def fill_weights(blocks, weight, flip):
    ch = weight.shape[2]
    zero = jnp.zeros((ch, ch), weight.dtype)
    for j in range(3):
        for b in range(2):
            for k in range(2):
                for n in range(2):
                    tap = 2 * b + k - n
                    ok = 0 <= tap <= 2
                    if flip:
                        value = weight[2 - tap, 2 - j] if ok else zero
                        blocks[j, b, n * ch : (n + 1) * ch, k * ch : (k + 1) * ch] = value
                    else:
                        value = weight[tap, j] if ok else zero
                        blocks[j, b, k * ch : (k + 1) * ch, n * ch : (n + 1) * ch] = value


def conv_pairs(taps, blocks, rows_out, cols, flip):
    dims = (((1,), (1,)), ((), ())) if flip else (((1,), (0,)), ((), ()))
    step = rows_out if flip else math.gcd(rows_out, 128)
    results = []
    for row in range(0, rows_out, step):
        total = None
        for j in range(3):
            for b in range(2):
                start = b * cols + row
                part = lax.dot_general(
                    taps[j][start : start + step], blocks[j, b], dims, preferred_element_type=F32
                )
                total = part if total is None else total + part
        results.append(total)
    return jnp.concatenate(results, 0)


def pick_halos(first, second, index, odd, times):
    one = first[index].astype(F32)
    two = second[index].astype(F32)
    upper = jnp.where(odd, one, two).astype(BF16)
    lower = jnp.where(odd, two, one).astype(BF16)
    return upper[:, None], lower[:, None]


def exponent(value):
    top = jnp.max(jnp.abs(value), axis=0, keepdims=True)
    return jnp.ceil(jnp.log2(jnp.maximum(top, 1e-30)))


def decays(log_decay):
    wide = jnp.concatenate([log_decay, log_decay], 1)
    times = wide.shape[0]
    sums = [wide[0:1]]
    for t in range(1, times):
        sums.append(sums[-1] + wide[t : t + 1])
    rate = [jnp.exp(wide[t : t + 1]) for t in range(times)]
    reach = [jnp.exp(total) for total in sums]
    tail = [jnp.exp(sums[-1] - total) for total in sums]
    return rate, reach, tail


def blocks_kernel(fields, weights, log_decay, blocks):
    fill_weights(blocks.at[0], weights.at[0], False)
    fill_weights(blocks.at[1], weights.at[1], True)


def blocks_call(fields, weights, log_decay):
    ch = weights.shape[3]
    return pl.pallas_call(
        blocks_kernel,
        out_shape=jax.ShapeDtypeStruct((2, 3, 2, 2 * ch, 2 * ch), BF16),
        compiler_params=pltpu.CompilerParams(vmem_limit_bytes=VMEM_LIMIT),
        cost_estimate=pl.CostEstimate(flops=0, bytes_accessed=10 << 20, transcendentals=0),
        name="blocks",
    )(fields, weights, log_decay)


def drive_kernel(
    place,
    fields,
    first,
    second,
    blocks,
    log_decay,
    states,
    adjoints,
    leaving,
    frame_taps,
    cot_taps,
    info,
    pairs,
):
    _, times, rows, cols, ch = fields.shape
    half = rows // 2
    odd = lax.rem(place[0], 2) == 1
    rate, reach, _ = decays(log_decay[...])
    results = ((states, frame_taps), (adjoints, cot_taps))
    for index, (result, taps_out) in enumerate(results):
        flip = index == 1
        top, bottom = pick_halos(first, second, index, odd, times)
        fill_pairs(pairs.at[index], fields.at[index], top, bottom)
        carry = None
        for step in range(times):
            t = times - 1 - step if flip else step
            taps = column_taps(pairs[index, t].reshape((half + 1) * cols, 2 * ch), cols)
            for j in range(3):
                taps_out[j, t] = taps[j]
            value = conv_pairs(taps, blocks.at[index], half * cols, cols, flip)
            if flip:
                value = value if carry is None else value + carry
                carry = rate[t] * value
            else:
                value = (1.0 - rate[t]) * value
                value = value if carry is None else rate[t] * carry + value
                carry = value
            result[t] = value
        if flip:
            leaving[...] = carry
        info[index : index + 1, :] = exponent(carry)
    total = reach[-1]
    high = total.astype(BF16).astype(F32)
    rest = (total - high) * 256.0
    middle = rest.astype(BF16).astype(F32)
    low = ((rest - middle) * 256.0).astype(BF16).astype(F32)
    info[2:3, :] = high
    info[3:4, :] = middle
    info[4:5, :] = low
    row = jnp.zeros((1, 2 * ch), F32)
    info[5:6, :] = row + lax.rem(place[1], 2).astype(F32)
    info[6:7, :] = row + lax.rem(lax.div(place[1], 2), 2).astype(F32)
    for d in range(info.shape[0] - 7):
        info[7 + d : 8 + d, :] = row + (lax.div(place[1], 4) ^ d).astype(F32)


def drive_call(place, fields, first, second, blocks, log_decay):
    _, times, rows, cols, ch = fields.shape
    half = rows // 2
    field = jax.ShapeDtypeStruct((times, half * cols, 2 * ch), F32)
    rows_info = (7 + lax.axis_size("tm") // 4 + 15) // 16 * 16
    taps = jax.ShapeDtypeStruct((3, times, (half + 1) * cols, 2 * ch), BF16)
    return pl.pallas_call(
        drive_kernel,
        in_specs=[pl.BlockSpec(memory_space=pltpu.SMEM)]
        + [pl.BlockSpec(memory_space=pltpu.VMEM)] * 5,
        out_shape=(
            field,
            field,
            jax.ShapeDtypeStruct(field.shape[1:], F32),
            taps,
            taps,
            jax.ShapeDtypeStruct((rows_info, 2 * ch), F32),
        ),
        scratch_shapes=[
            pltpu.VMEM((2, times, half + 1, cols, 2 * ch), BF16),
        ],
        compiler_params=pltpu.CompilerParams(vmem_limit_bytes=VMEM_LIMIT),
        cost_estimate=pl.CostEstimate(
            flops=times * rows * cols * ch * ch * 48, bytes_accessed=12 << 20, transcendentals=0
        ),
        name="drive",
    )(place, fields, first, second, blocks, log_decay)


def grads_kernel(
    place,
    states,
    adjoints,
    state_in,
    adjoint_in,
    log_decay,
    frame_taps,
    cot_taps,
    states_bf,
    inflow_bf,
    first,
    second,
    grads_in,
    grads_out,
    info,
    turned,
):
    times, count, width = states.shape
    ch = width // 2
    cols = frame_taps.shape[2] - count
    odd = lax.rem(place[0], 2) == 1
    rate, reach, tail = decays(log_decay[...])
    add = state_in[...]
    back = adjoint_in[...]
    for t in range(times):
        value = (states[t] + reach[t] * add).astype(BF16)
        states_bf[t] = value
        turned[0, t] = value.T
        value = ((1.0 - rate[t]) * (adjoints[t] + tail[t] * back)).astype(BF16)
        inflow_bf[t] = value
        turned[1, t] = value.T
        for index, field in enumerate((states_bf, inflow_bf)):
            low = field[t, :cols, :ch].astype(F32)
            high = field[t, count - cols :, ch:].astype(F32)
            first[index, t] = jnp.where(odd, low, high).astype(BF16)
            second[index, t] = jnp.where(odd, high, low).astype(BF16)
    for index, (taps, grads) in enumerate(((cot_taps, grads_out), (frame_taps, grads_in))):
        largest = None
        for j in range(3):
            blocks = []
            for b in range(2):
                total = None
                for t in range(times):
                    part = jnp.dot(
                        turned[index, t],
                        taps[j, t, b * cols : b * cols + count],
                        preferred_element_type=F32,
                    )
                    total = part if total is None else total + part
                blocks.append(total)
            for tap in range(3):
                total = None
                for b in range(2):
                    for c in range(2):
                        a = 2 * b + c - tap
                        if a in (0, 1):
                            part = blocks[b][a * ch : (a + 1) * ch, c * ch : (c + 1) * ch]
                            total = part if total is None else total + part
                if index == 0:
                    spot = (2 - tap) * 3 + 2 - j
                else:
                    spot = tap * 3 + j
                    total = total.T
                grads[spot * ch : (spot + 1) * ch, :] = total
                top = jnp.max(jnp.abs(total), axis=0, keepdims=True)
                largest = top if largest is None else jnp.maximum(largest, top)
        info[index : index + 1, :] = exponent(largest)
    row = jnp.zeros((1, ch), F32)
    info[2:3, :] = row + lax.rem(place[0], 2).astype(F32)
    info[3:4, :] = row + lax.rem(place[1], 2).astype(F32)
    info[4:5, :] = row + lax.rem(lax.div(place[0], 2), 2).astype(F32)
    info[5:, :] = jnp.zeros((info.shape[0] - 5, ch), F32)


def grads_call(place, states, adjoints, state_in, adjoint_in, log_decay, frame_taps, cot_taps):
    times, count, width = states.shape
    ch = width // 2
    cols = frame_taps.shape[2] - count
    field = jax.ShapeDtypeStruct((times, count, width), BF16)
    edge = jax.ShapeDtypeStruct((2, times, cols, ch), BF16)
    grads = jax.ShapeDtypeStruct((9 * ch, ch), F32)
    return pl.pallas_call(
        grads_kernel,
        in_specs=[pl.BlockSpec(memory_space=pltpu.SMEM)]
        + [pl.BlockSpec(memory_space=pltpu.VMEM)] * 7,
        out_shape=(field, field, edge, edge, grads, grads, jax.ShapeDtypeStruct((16, ch), F32)),
        scratch_shapes=[pltpu.VMEM((2, times, width, count), BF16)],
        compiler_params=pltpu.CompilerParams(vmem_limit_bytes=VMEM_LIMIT),
        cost_estimate=pl.CostEstimate(
            flops=times * count * ch * ch * 96, bytes_accessed=12 << 20, transcendentals=0
        ),
        name="grads",
    )(place, states, adjoints, state_in, adjoint_in, log_decay, frame_taps, cot_taps)


def output_kernel(
    place, field, first, second, weight, skip, direct, out, pairs, blocks, near, sems, *, flip
):
    times, half, cols, width = field.shape
    ch = width // 2
    fill_weights(blocks, weight, flip)
    top, bottom = pick_halos(first, second, int(flip), lax.rem(place[0], 2) == 1, times)
    fill_pairs_from_pairs(pairs, field, top, bottom)
    gain = skip[...]
    stores = []
    for t in range(times):
        taps = column_taps(pairs[t].reshape((half + 1) * cols, width), cols)
        value = conv_pairs(taps, blocks, half * cols, cols, flip).reshape(half, cols, width)
        for i in range(half):
            for c in range(2):
                base = gain * direct[t, 2 * i + c].astype(F32)
                near[t, 2 * i + c] = (value[i, :, c * ch : (c + 1) * ch] + base).astype(BF16)
        stores.append(pltpu.make_async_copy(near.at[t], out.at[t], sems.at[t]))
        stores[-1].start()
    for copy in stores:
        copy.wait()


def output_call(place, field, first, second, weight, skip, direct, flip):
    times, half, cols, width = field.shape
    ch = width // 2
    return pl.pallas_call(
        functools.partial(output_kernel, flip=flip),
        in_specs=[pl.BlockSpec(memory_space=pltpu.SMEM)]
        + [pl.BlockSpec(memory_space=pltpu.VMEM)] * 6,
        out_specs=pl.BlockSpec(memory_space=pltpu.HBM),
        out_shape=jax.ShapeDtypeStruct(direct.shape, BF16),
        scratch_shapes=[
            pltpu.VMEM((times, half + 1, cols, width), BF16),
            pltpu.VMEM((3, 2, width, width), BF16),
            pltpu.VMEM(direct.shape, BF16),
            pltpu.SemaphoreType.DMA((times,)),
        ],
        compiler_params=pltpu.CompilerParams(vmem_limit_bytes=VMEM_LIMIT),
        cost_estimate=pl.CostEstimate(
            flops=times * half * cols * ch * ch * 48, bytes_accessed=4 << 20, transcendentals=0
        ),
        name="grad_frames" if flip else "output",
    )(place, field, first, second, weight, skip, direct)


def swap(value, tm_bits, tile_bits):
    tiles = lax.axis_size("tile")
    mask = tm_bits * tiles + tile_bits
    count = lax.axis_size("tm") * tiles
    return lax.ppermute(value, ("tm", "tile"), [(i, i ^ mask) for i in range(count)])


def swap_across(value):
    count = lax.axis_size("tile")
    pairs = []
    for i in range(1, count - 1, 2):
        pairs += [(i, i + 1), (i + 1, i)]
    return lax.ppermute(value, "tile", pairs)


def laid(parts, count):
    total, start = None, 0
    for part in parts:
        end = count - start - part.shape[0]
        wide = jnp.pad(part, ((start, end), (0, 0)))
        total = wide if total is None else total + wide
        start += part.shape[0]
    return total


def packed(value, scale, *rows):
    parts = [value * jnp.exp2(-scale), *rows]
    return laid(parts, value.shape[0] + 16).astype(jnp.float16)


def whole_decay(rows):
    return rows[0:1] + rows[1:2] / 256.0 + rows[2:3] / 65536.0


def by_place(values, flags):
    values = list(values)
    for n, flag in enumerate(flags):
        for d in range(len(values)):
            if not d >> n & 1:
                a, b = values[d], values[d + 2**n]
                values[d], values[d + 2**n] = jnp.where(flag, b, a), jnp.where(flag, a, b)
    return values


def carry_over(state_end, adjoint_end, info):
    squares = lax.axis_size("tm") // 4
    flags = [info[5:6] > 0.5, info[6:7] > 0.5]
    places = [info[7 + d : 8 + d] for d in range(squares)]
    part = state_end.shape[0] // 4
    width = state_end.shape[1]

    def both(low, high, scale_low, scale_high, rows):
        parts = [low * jnp.exp2(-scale_low), high * jnp.exp2(-scale_high), rows]
        return laid(parts, 2 * part + 16).astype(jnp.float16)

    def quarters(value):
        return by_place([value[n * part : (n + 1) * part] for n in range(4)], flags)

    states, adjoints = quarters(state_end), quarters(adjoint_end)
    messages = [both(states[d], adjoints[d], info[0:1], info[1:2], info[:5]) for d in (1, 2, 3)]
    received = [swap(m, d + 1, 0).astype(F32) for d, m in enumerate(messages)]
    rows = [info[:5]] + [got[2 * part : 2 * part + 5] for got in received]
    state_scale = functools.reduce(jnp.maximum, [row[0:1] for row in rows])
    adjoint_scale = functools.reduce(jnp.maximum, [row[1:2] for row in rows])
    states = [states[0]] + [
        got[:part] * jnp.exp2(row[0:1]) for got, row in zip(received, rows[1:])
    ]
    adjoints = [adjoints[0]] + [
        got[part : 2 * part] * jnp.exp2(row[1:2]) for got, row in zip(received, rows[1:])
    ]
    states, adjoints = by_place(states, flags), by_place(adjoints, flags)
    decay_rows = by_place([row[2:5] for row in rows], flags)
    totals = [whole_decay(row) for row in decay_rows]

    one = jnp.ones((1, width), F32)
    zero = jnp.zeros((part, width), F32)
    before, reach = [zero], [one]
    for n in range(4):
        before.append(totals[n] * before[-1] + states[n])
        reach.append(reach[-1] * totals[n])
    after, back = [zero], [one]
    for n in (3, 2, 1, 0):
        after.insert(0, adjoints[n] + totals[n] * after[0])
        back.insert(0, back[0] * totals[n])
    state_square, adjoint_square = before.pop(), after.pop(0)
    back.pop(0)

    messages = []
    bit = 1
    while bit < squares:
        later = places[bit] < places[0]
        scale = jnp.where(later, adjoint_scale, state_scale)
        value = jnp.where(later, adjoint_square, state_square)
        messages.append(packed(value, scale, scale, *decay_rows))
        bit *= 2
    through_square, values = {}, {}
    top_scale = jnp.maximum(state_scale, adjoint_scale)
    for d in range(1, squares):
        got = swap(messages[d.bit_length() - 1], 4 * d, 0).astype(F32)
        there = [got[part + 1 + 3 * n : part + 4 + 3 * n] for n in range(4)]
        through_square[d] = functools.reduce(jnp.multiply, [whole_decay(row) for row in there])
        values[d] = got[:part] * jnp.exp2(got[part : part + 1])
        top_scale = jnp.maximum(top_scale, got[part : part + 1])
    state_before, adjoint_after = zero, zero
    for d in values:
        term = values[d]
        if squares > 2:
            through = one
            for e in values:
                low = jnp.minimum(places[0], places[d])
                high = jnp.maximum(places[0], places[d])
                inside = (low < places[e]) & (places[e] < high)
                through = through * jnp.where(inside, through_square[e], 1.0)
            term = through * term
        state_before = state_before + jnp.where(places[d] < places[0], term, 0.0)
        adjoint_after = adjoint_after + jnp.where(places[d] > places[0], term, 0.0)

    states = by_place([before[n] + reach[n] * state_before for n in range(4)], flags)
    adjoints = by_place([after[n] + back[n] * adjoint_after for n in range(4)], flags)
    messages = [both(states[d], adjoints[d], top_scale, top_scale, top_scale) for d in (1, 2, 3)]
    received = [swap(m, d + 1, 0).astype(F32) for d, m in enumerate(messages)]
    scales = [jnp.exp2(got[2 * part : 2 * part + 1]) for got in received]
    states = [states[0]] + [got[:part] * s for got, s in zip(received, scales)]
    adjoints = [adjoints[0]] + [got[part : 2 * part] * s for got, s in zip(received, scales)]
    return (
        jnp.concatenate(by_place(states, flags), 0),
        jnp.concatenate(by_place(adjoints, flags), 0),
    )


def unpacked(got):
    rows = got.shape[-2] - 16
    wide = got.astype(F32)
    scale = wide[..., rows : rows + 1, :]
    return wide[..., :rows, :] * jnp.exp2(scale), scale


def shards(frames, cotangent, w_in, w_out, skip, log_decay):
    times, rows, cols, ch = frames.shape
    half = rows // 2
    place = jnp.stack([lax.axis_index("tile"), lax.axis_index("tm")]).astype(jnp.int32)
    place = lax.optimization_barrier(place)
    odd = place[0] % 2 == 1
    gain = skip[None, :]

    low = jnp.stack([frames[:, 0], cotangent[:, 0]])
    high = jnp.stack([frames[:, -1], cotangent[:, -1]])
    second = swap_across(jnp.where(odd, high, low))
    first = swap(jnp.where(odd, low, high), 0, 1)

    fields = jnp.stack([frames, cotangent])
    blocks = blocks_call(fields, jnp.stack([w_in, w_out]), log_decay)
    states, adjoints, leaving, frame_taps, cot_taps, info = drive_call(
        place, fields, first, second, blocks, log_decay
    )
    state_in, adjoint_in = carry_over(states[-1], leaving, info)
    states_bf, inflow_bf, first, second, in_part, out_part, info = grads_call(
        place, states, adjoints, state_in, adjoint_in, log_decay, frame_taps, cot_taps
    )

    out_scale, in_scale = info[0:1], info[1:2]
    odd, odd_tm, high_tile = (info[n : n + 1] > 0.5 for n in (2, 3, 4))
    scale = jnp.where(odd, in_scale, out_scale)
    message = packed(jnp.where(odd, in_part, out_part), scale, scale)
    message, first, second = lax.optimization_barrier((message, first, second))
    got, got_scale = unpacked(swap(message, 0, 1))
    value = jnp.where(odd, out_part, in_part) + got
    scale = jnp.maximum(jnp.where(odd, out_scale, in_scale), got_scale)
    second = swap_across(second)
    first = swap(first, 0, 1)

    bits = [((1, 0), odd_tm), ((0, 2), high_tile)] if lax.axis_size("tile") > 2 else [((1, 0), odd_tm)]
    parts = 2 ** len(bits)
    pieces = list(value.reshape(parts, -1, ch))
    for n, (_, high) in enumerate(bits):
        for d in range(parts):
            if not d >> n & 1:
                a, b = pieces[d], pieces[d + 2**n]
                pieces[d], pieces[d + 2**n] = jnp.where(high, b, a), jnp.where(high, a, b)

    def mask(d):
        chosen = [bit for n, (bit, _) in enumerate(bits) if d >> n & 1]
        return sum(b[0] for b in chosen), sum(b[1] for b in chosen)

    messages = [packed(pieces[d], scale, scale) for d in range(1, parts)]
    value = pieces[0]
    states_bf = states_bf.reshape(times, half, cols, 2 * ch)
    inflow_bf = inflow_bf.reshape(times, half, cols, 2 * ch)
    *messages, states_bf = lax.optimization_barrier((*messages, states_bf))
    received = [swap(m, *mask(d + 1)) for d, m in enumerate(messages)]
    for got in received:
        got, got_scale = unpacked(got)
        value = value + got
        scale = jnp.maximum(scale, got_scale)

    left = []
    bit = 2
    while bit < lax.axis_size("tm"):
        left.append((bit, 0))
        bit *= 2
    bit = 4
    while bit < lax.axis_size("tile"):
        left.append((0, bit))
        bit *= 2
    waiting = inflow_bf
    for n in range(0, len(left), 2):
        group = left[n : n + 2]
        message = packed(value, scale, scale)
        message, states_bf, waiting = lax.optimization_barrier((message, states_bf, waiting))
        terms = [message]
        for d in range(1, 2 ** len(group)):
            chosen = [b for k, b in enumerate(group) if d >> k & 1]
            terms.append(swap(message, sum(b[0] for b in chosen), sum(b[1] for b in chosen)))
        terms = [unpacked(term) for term in terms]
        while len(terms) > 1:
            terms = [
                (a[0] + b[0], jnp.maximum(a[1], b[1])) for a, b in zip(terms[::2], terms[1::2])
            ]
        value, scale = terms[0]

    output = output_call(place, states_bf, first, second, w_out, gain, frames, False)

    message = packed(value, scale, scale)
    message, output, waiting = lax.optimization_barrier((message, output, waiting))
    gathered = [message] + [swap(message, *mask(d)) for d in range(1, parts)]
    grad_frames = output_call(place, waiting, first, second, w_in, gain, cotangent, True)
    for _, high in bits:
        gathered = [
            (jnp.where(high, b, a), jnp.where(high, a, b))
            for a, b in zip(gathered[::2], gathered[1::2])
        ]
        gathered = [jnp.concatenate(pair, 0) for pair in gathered]
    (mine,) = gathered
    mine, grad_frames = lax.optimization_barrier((mine, grad_frames))
    theirs = swap(mine, 0, 1)
    factor = 1.0 / math.sqrt(
        times * lax.axis_size("tm") * rows * lax.axis_size("tile") * cols
    )
    mine, _ = unpacked(mine.reshape(parts, -1, ch))
    theirs, _ = unpacked(theirs.reshape(parts, -1, ch))
    results = [
        (jnp.where(odd, a, b) * factor).reshape(3, 3, ch, ch)
        for a, b in ((theirs, mine), (mine, theirs))
    ]
    return (output, grad_frames, results[0], results[1])


def solution(mesh):
    placed = (
        P("tm", "tile", None, None),
        P("tm", "tile", None, None),
        P(),
        P(),
        P(),
        P("tm", None),
    )
    return jax.shard_map(
        shards,
        mesh=mesh,
        in_specs=placed,
        out_specs=(P("tm", "tile", None, None), P("tm", "tile", None, None), P(), P()),
        check_vma=False,
    )
```
